32 devices in a mesh: seq: 16 (over z, y, x), head: 2 (over core).
Axes of the slice: x: 2, y: 2, z: 4, core: 2. Of those that a mesh axis runs over, the one named last changes fastest.
Arguments:
- queries: bfloat16 [4096, 4096], P('seq', 'head'), may hold values from -6 to 6
- key_rows: bfloat16 [4096, 4096], P('seq', 'head'), may hold values from -6 to 6
- value_rows: bfloat16 [4096, 4096], P('seq', 'head'), may hold values from -180 to 180
- window: int32 [64, 12], P('seq'), may hold values from 0 to 63, as said below
- random_blocks: int32 [64, 3], P('seq'), may hold values from 0 to 63, as said below
- global_blocks: int32 [2], replicated, may hold values from 0 to 63, as said below
- norm_gain: float32 [4096], P('head'), may hold values from 0.25 to 1.75
Outputs:
- normed: bfloat16 [4096, 4096], P('seq', 'head')
The draws below stay inside these ranges and needn't reach their ends.
Inputs may be any that keep to these rules, and one draw needn't show every extreme that they name: `window`: row b names 12 distinct blocks, each with (id - b) mod 64 within 8 of 0 either way around the circle; b itself, b - 8 and b + 8 (mod 64) are always among them. `random_blocks`: shard s holds blocks s * 4 to s * 4 + 3. The 12 entries of the rows of one device name each shard at most 1 times; one shard is named exactly 1 times by the rows of every device. `global_blocks`: distinct blocks; one of them is the last block of the sequence, 63.
All inputs are finite; a program needn't handle non-finite values.
Results may differ from the reference program's by a relative error of at most 0.0045.
Values may be sent and summed in bfloat16 or wider, within the bound.
No kernel may reach another device: no remote copies, remote signals or barrier semaphores. Data moves between devices by JAX's collectives and lax.ppermute only.
A program may use at most 128 MiB of HBM per device.

```python
import math
import jax
import jax.numpy as jnp
from jax import lax

HEADS = 32
HD = 128
D = 4096
BLK = 64
BLK_DEV = 4
RAND = 3
SEQ = 4096
NBLK = 64
REACH = 8
WIN = 12
SLOTS = 1


def draw_queries(key, part):
    base = jnp.clip(jax.random.normal(jax.random.fold_in(key, 1), (SEQ, D), jnp.float32), -6.0, 6.0)
    return base.astype(jnp.bfloat16)


def draw_key_rows(key, part):
    base = jnp.clip(jax.random.normal(jax.random.fold_in(key, 2), (SEQ, D), jnp.float32), -6.0, 6.0)
    return base.astype(jnp.bfloat16)


def draw_value_rows(key, part):
    head_of = (jnp.arange(D, dtype=jnp.int32) // HD).astype(jnp.float32)
    spread = head_of / max(HEADS - 1, 1)
    row_scale = jnp.exp(jax.random.uniform(jax.random.fold_in(key, 5), (SEQ, 1), jnp.float32, 0.0, math.log(10.0)))
    base = jnp.clip(jax.random.normal(jax.random.fold_in(key, 4), (SEQ, D), jnp.float32), -6.0, 6.0)
    column_scale = 1.0 + 2.0 * spread
    return (base * column_scale[None, :] * row_scale).astype(jnp.bfloat16)


def draw_window(key, part):
    middle = jnp.concatenate([jnp.arange(-REACH + 1, 0), jnp.arange(1, REACH)]).astype(jnp.int32)
    pick_keys = jax.random.split(jax.random.fold_in(key, 1), NBLK)
    picked = jax.vmap(lambda one_key: jax.random.permutation(one_key, middle)[:WIN - 3])(pick_keys)
    edges = jnp.broadcast_to(jnp.array([0, -REACH, REACH], dtype=jnp.int32), (NBLK, 3))
    offsets = jnp.concatenate([edges, picked.astype(jnp.int32)], axis=1)
    order_keys = jax.random.split(jax.random.fold_in(key, 2), NBLK)
    orders = jax.vmap(lambda one_key: jax.random.permutation(one_key, WIN))(order_keys)
    offsets = jnp.take_along_axis(offsets, orders, axis=1)
    block_ids = jnp.arange(NBLK, dtype=jnp.int32)[:, None]
    return ((block_ids + offsets) % NBLK).astype(jnp.int32)


def draw_random_blocks(key, part):
    used_count = BLK_DEV * RAND
    slot_total = NBLK // BLK_DEV * SLOTS
    shard_total = NBLK // BLK_DEV
    common_shard = jax.random.randint(jax.random.fold_in(key, 1), (), 0, shard_total)
    owner_keys = jax.random.split(jax.random.fold_in(key, 2), shard_total)
    shuffled = jax.vmap(lambda one_key: jax.random.permutation(one_key, slot_total))(owner_keys).astype(jnp.int32)
    shard_of = shuffled // SLOTS
    grouping = jnp.where(shard_of == common_shard, 0, 1).astype(jnp.int32)
    ordering = jnp.argsort(grouping, axis=1, stable=True)
    chosen = jnp.take_along_axis(shard_of, ordering, axis=1)[:, :used_count]
    mix_keys = jax.random.split(jax.random.fold_in(key, 3), shard_total)
    mixing = jax.vmap(lambda one_key: jax.random.permutation(one_key, used_count))(mix_keys)
    chosen = jnp.take_along_axis(chosen, mixing, axis=1)
    within = jax.random.randint(jax.random.fold_in(key, 4), (shard_total, used_count), 0, BLK_DEV)
    return (chosen * BLK_DEV + within).reshape(NBLK, RAND).astype(jnp.int32)


def draw_global_blocks(key, part):
    other_block = jax.random.randint(jax.random.fold_in(key, 1), (), 0, NBLK - 1).astype(jnp.int32)
    last_block = jnp.array(NBLK - 1, dtype=jnp.int32)
    flipped = jax.random.randint(jax.random.fold_in(key, 2), (), 0, 2).astype(jnp.int32)
    first = jnp.where(flipped == 1, other_block, last_block)
    second = jnp.where(flipped == 1, last_block, other_block)
    return jnp.stack([first, second]).astype(jnp.int32)


def setup_inputs(seed: int = 0) -> dict:
    key_list = jax.random.split(jax.random.key(seed), 8)
    queries = draw_queries(jax.random.fold_in(key_list[7], 71), 0)
    key_rows = draw_key_rows(jax.random.fold_in(key_list[7], 71), 0)
    value_rows = draw_value_rows(jax.random.fold_in(key_list[7], 71), 0)
    window = draw_window(jax.random.fold_in(key_list[7], 71), 0)
    random_blocks = draw_random_blocks(jax.random.fold_in(key_list[7], 71), 0)
    global_blocks = draw_global_blocks(jax.random.fold_in(key_list[7], 71), 0)
    norm_gain = jnp.clip(1.0 + 0.15 * jax.random.normal(key_list[6], (D,), jnp.float32), 0.25, 1.75)
    return dict(queries=queries, key_rows=key_rows, value_rows=value_rows, window=window, random_blocks=random_blocks, global_blocks=global_blocks, norm_gain=norm_gain)


def source_part(query_set, key_set, value_set, head_count):
    item_count, row_count, row_width = query_set.shape
    head_size = row_width // head_count
    query_heads = query_set.reshape(item_count, row_count, head_count, head_size).astype(jnp.float32)
    key_heads = key_set.reshape(item_count, key_set.shape[1], head_count, head_size).astype(jnp.float32)
    value_heads = value_set.reshape(item_count, value_set.shape[1], head_count, head_size).astype(jnp.float32)
    scores = jnp.einsum('nqhd,nkhd->nhqk', query_heads, key_heads) * head_size ** (-0.5)
    maxima = lax.optimization_barrier(jnp.max(scores, axis=-1))
    lifted = jnp.exp(scores - maxima[..., None])
    totals = lax.optimization_barrier(jnp.sum(lifted, axis=-1))
    weights = lax.optimization_barrier(lifted.astype(jnp.bfloat16)).astype(jnp.float32)
    summed = jnp.einsum('nhqk,nkhd->nqhd', weights, value_heads)
    return (maxima, totals, summed.reshape(item_count, row_count, row_width))

def merge_sources(maxima, totals, partial_sums, head_count):
    overall = lax.optimization_barrier(jnp.max(maxima, axis=0))
    factor = jnp.exp(maxima - overall[None])
    denominator = lax.optimization_barrier(jnp.sum(factor * totals, axis=0))
    item_count, row_count, row_width = partial_sums.shape
    split_sums = partial_sums.reshape(item_count, row_count, head_count, row_width // head_count)
    weighted = lax.optimization_barrier(jnp.sum(split_sums * jnp.transpose(factor, (0, 2, 1))[..., None], axis=0))
    return (weighted / jnp.transpose(denominator)[..., None]).reshape(row_count, row_width)

def reference(queries, key_rows, value_rows, window, random_blocks, global_blocks, norm_gain):
    row_width = queries.shape[1]
    head_count = row_width // HD
    query_blocks = queries.reshape(NBLK, BLK, row_width)
    key_blocks = key_rows.reshape(NBLK, BLK, row_width)
    value_blocks = value_rows.reshape(NBLK, BLK, row_width)

    def one_block(block_id):
        one_query = lax.dynamic_index_in_dim(query_blocks, block_id, 0, keepdims=True)
        near_ids = jnp.concatenate([lax.dynamic_index_in_dim(window, block_id, 0, keepdims=False).astype(jnp.int32), global_blocks.astype(jnp.int32)])
        near_keys = jnp.take(key_blocks, near_ids, axis=0).reshape(1, -1, row_width)
        near_values = jnp.take(value_blocks, near_ids, axis=0).reshape(1, -1, row_width)
        near_max, near_total, near_sum = source_part(one_query, near_keys, near_values, head_count)
        rand_ids = lax.dynamic_index_in_dim(random_blocks, block_id, 0, keepdims=False).astype(jnp.int32)
        rand_keys = jnp.take(key_blocks, rand_ids, axis=0)
        rand_values = jnp.take(value_blocks, rand_ids, axis=0)
        repeated = jnp.broadcast_to(one_query, (rand_ids.shape[0], BLK, row_width))
        rand_max, rand_total, rand_sum = source_part(repeated, rand_keys, rand_values, head_count)
        return merge_sources(jnp.concatenate([near_max, rand_max]), jnp.concatenate([near_total, rand_total]), jnp.concatenate([near_sum, rand_sum]), head_count)
    attended = lax.map(one_block, jnp.arange(NBLK, dtype=jnp.int32)).reshape(SEQ, row_width)
    row_squares = lax.optimization_barrier(jnp.sum(attended * attended, axis=1))
    inverse = lax.rsqrt(row_squares / D + 1e-06)
    return (attended * inverse[:, None] * norm_gain[None, :]).astype(jnp.bfloat16)
```

```python
from functools import partial
import math

import jax
import jax.numpy as jnp
from jax import lax
from jax.experimental import pallas as pl
from jax.experimental.pallas import tpu as pltpu
from jax.sharding import PartitionSpec as P

HD = 128
D = 4096
BLK = 64
PLANE = 4
CHUNKS = 2
ABSENT = -1e30
VMEM = 40 * 2**20


def up_to(rows, multiple):
    return -(-rows // multiple) * multiple


def exchange(array, shards, flip):
    return lax.ppermute(array, "seq", [(i, i ^ flip) for i in range(shards)])


def along(array, shards, step, first, last):
    pairs = [(z * PLANE + c, (z + step) * PLANE + c) for z in range(first, last) for c in range(PLANE)]
    return lax.ppermute(array, "seq", pairs)


def split_lse(lse):
    high = lse.astype(jnp.bfloat16).astype(jnp.float32)
    rest = lse - high
    middle = rest.astype(jnp.bfloat16).astype(jnp.float32)
    low = rest - middle
    return jnp.concatenate([high, middle, low, jnp.zeros_like(low)], axis=0).astype(jnp.bfloat16)


def join_lse(packed):
    rows = packed.shape[0] // 4
    pieces = packed.astype(jnp.float32)
    return pieces[:rows] + pieces[rows : 2 * rows] + pieces[2 * rows : 3 * rows]


def attend(planes, heads, plane_ref, bias_ref, *refs):
    queries = refs[: 2 * planes - 1]
    pairs = refs[2 * planes - 1 : 2 * planes - 1 + PLANE]
    outs = refs[2 * planes - 1 + PLANE : -1]
    messages, own_ref, own_lse_ref = outs[: planes - 1], outs[planes - 1], outs[planes]
    lse_ref = refs[-1]
    head = pl.program_id(0)
    plane = plane_ref[0]
    scale = HD**-0.5 * math.log2(math.e)
    shard_rows = pairs[0].shape[1]
    blocks = shard_rows // BLK
    for slot in range(planes):
        if slot == 0:
            query = queries[0][...]
        else:
            query = jnp.where(plane + slot < planes, queries[planes - 1 + slot][...], queries[planes - slot][...])
        tiles = []
        for j in range(PLANE):
            scores = lax.dot_general(pairs[j][0], query, (((1,), (1,)), ((), ())), preferred_element_type=jnp.float32)
            bias = bias_ref[slot, j * blocks : (j + 1) * blocks, :]
            lifted = scores.reshape(blocks, BLK, -1) * scale + bias[:, None, :]
            tiles.append(lifted.reshape(shard_rows, -1))
        peak = jnp.max(tiles[0], axis=0, keepdims=True)
        for j in range(1, PLANE):
            peak = jnp.maximum(peak, jnp.max(tiles[j], axis=0, keepdims=True))
        total, part = 0.0, 0.0
        for j in range(PLANE):
            weight = jnp.exp2(tiles[j] - peak)
            total = total + jnp.sum(weight, axis=0, keepdims=True)
            part = part + lax.dot_general(
                pairs[j][1], weight.astype(jnp.bfloat16), (((0,), (0,)), ((), ())), preferred_element_type=jnp.float32
            )
        part = part * (1.0 / total)
        lse_ref[slot, pl.ds(head, 1), :] = peak + jnp.log2(total)
        if slot == 0:
            own_ref[...] = part
        else:
            messages[slot - 1][pl.ds(pl.multiple_of(head * HD, HD), HD), :] = part.astype(jnp.bfloat16)

    @pl.when(head == heads - 1)
    def _():
        own_lse_ref[...] = lse_ref[0]
        for slot in range(1, planes):
            messages[slot - 1][heads * HD :, :] = split_lse(lse_ref[slot])


def attention(plane, bias, own, ups, downs, pairs):
    rows, width = own.shape
    heads, planes = width // HD, len(ups) + 1
    lse_rows = up_to(heads, 8)
    query_spec = pl.BlockSpec((rows, HD), lambda h, s: (0, h))
    pair_spec = pl.BlockSpec((2, rows, HD), lambda h, s: (0, 0, h))
    message = jax.ShapeDtypeStruct((width + 4 * lse_rows, rows), jnp.bfloat16)
    message_spec = pl.BlockSpec(message.shape, lambda h, s: (0, 0))
    products = heads * planes * PLANE * rows * rows
    return pl.pallas_call(
        partial(attend, planes, heads),
        out_shape=[message] * (planes - 1)
        + [jax.ShapeDtypeStruct((width, rows), jnp.float32), jax.ShapeDtypeStruct((lse_rows, rows), jnp.float32)],
        grid_spec=pltpu.PrefetchScalarGridSpec(
            num_scalar_prefetch=1,
            grid=(heads,),
            in_specs=[pl.BlockSpec(bias.shape, lambda h, s: (0, 0, 0))]
            + [query_spec] * (2 * planes - 1)
            + [pair_spec] * PLANE,
            out_specs=[message_spec] * (planes - 1)
            + [
                pl.BlockSpec((HD, rows), lambda h, s: (h, 0)),
                pl.BlockSpec((lse_rows, rows), lambda h, s: (0, 0)),
            ],
            scratch_shapes=[pltpu.VMEM((planes, lse_rows, rows), jnp.float32)],
        ),
        cost_estimate=pl.CostEstimate(
            flops=4 * products * HD, bytes_accessed=8 * 2**20, transcendentals=products
        ),
        compiler_params=pltpu.CompilerParams(vmem_limit_bytes=VMEM),
        name="attention",
    )(plane, bias, own, *ups, *downs, *pairs)


def merge(planes, heads, plane_ref, *refs):
    plane = plane_ref[0]
    for mine, came, out, valid in (
        (refs[0], refs[1], refs[4], plane > 0),
        (refs[2], refs[3], refs[5], plane < planes - 1),
    ):
        mine_lse = join_lse(mine[heads * HD :, :])
        came_lse = jnp.where(valid, join_lse(came[heads * HD :, :]), ABSENT)
        peak = jnp.maximum(mine_lse, came_lse)
        mine_weight, came_weight = jnp.exp2(mine_lse - peak), jnp.exp2(came_lse - peak)
        total = mine_weight + came_weight
        mine_weight, came_weight = mine_weight / total, came_weight / total
        for head in range(heads):
            at = slice(head * HD, (head + 1) * HD)
            mixed = mine[at, :].astype(jnp.float32) * mine_weight[head : head + 1]
            mixed += came[at, :].astype(jnp.float32) * came_weight[head : head + 1]
            out[at, :] = mixed.astype(jnp.bfloat16)
        out[heads * HD :, :] = split_lse(peak + jnp.log2(total))


def merged(plane, planes, heads, *messages):
    spec = pl.BlockSpec(memory_space=pltpu.VMEM)
    size = math.prod(messages[0].shape)
    return pl.pallas_call(
        partial(merge, planes, heads),
        out_shape=[jax.ShapeDtypeStruct(messages[0].shape, jnp.bfloat16)] * 2,
        in_specs=[pl.BlockSpec(memory_space=pltpu.SMEM)] + [spec] * 4,
        out_specs=[spec] * 2,
        cost_estimate=pl.CostEstimate(flops=8 * size, bytes_accessed=12 * size, transcendentals=0),
        compiler_params=pltpu.CompilerParams(vmem_limit_bytes=VMEM),
        name="merge",
    )(plane, *messages)


def finish(planes, heads, plane_ref, own_ref, own_lse_ref, up_ref, down_ref, gain_ref, out_ref, squares_ref):
    plane = plane_ref[0]
    own_lse = own_lse_ref[...]
    up_lse = jnp.where(plane > 0, join_lse(up_ref[heads * HD :, :]), ABSENT)
    down_lse = jnp.where(plane < planes - 1, join_lse(down_ref[heads * HD :, :]), ABSENT)
    peak = jnp.maximum(own_lse, jnp.maximum(up_lse, down_lse))
    weights = [jnp.exp2(lse - peak) for lse in (own_lse, up_lse, down_lse)]
    total = weights[0] + weights[1] + weights[2]
    weights = [weight / total for weight in weights]
    squares = 0.0
    for head in range(heads):
        at = slice(head * HD, (head + 1) * HD)
        row = slice(head, head + 1)
        mixed = own_ref[at, :] * weights[0][row]
        mixed += up_ref[at, :].astype(jnp.float32) * weights[1][row]
        mixed += down_ref[at, :].astype(jnp.float32) * weights[2][row]
        squares += jnp.sum(mixed * mixed, axis=0, keepdims=True)
        out_ref[:, at] = mixed.T * gain_ref[:, at]
    squares_ref[...] = squares


def finished(plane, planes, heads, own, own_lse, up, down, gain):
    spec = pl.BlockSpec(memory_space=pltpu.VMEM)
    width, rows = own.shape
    return pl.pallas_call(
        partial(finish, planes, heads),
        out_shape=[
            jax.ShapeDtypeStruct((rows, width), jnp.float32),
            jax.ShapeDtypeStruct((1, rows), jnp.float32),
        ],
        in_specs=[pl.BlockSpec(memory_space=pltpu.SMEM)] + [spec] * 5,
        out_specs=[spec] * 2,
        cost_estimate=pl.CostEstimate(flops=8 * own.size, bytes_accessed=12 * own.size, transcendentals=0),
        compiler_params=pltpu.CompilerParams(vmem_limit_bytes=VMEM),
        name="finish",
    )(plane, own, own_lse, up, down, gain)


def count_bias(window, random_blocks, global_blocks, position, shards):
    per_device = window.shape[0]
    planes = shards // PLANE
    plane, corner = position // PLANE, position % PLANE
    named = lax.all_gather(jnp.concatenate([window, random_blocks], axis=1), "seq")
    slots = (plane + jnp.arange(planes, dtype=jnp.int32)) % planes
    named = jnp.take(named, slots * PLANE + corner, axis=0)
    owners = plane * PLANE + (corner ^ jnp.arange(PLANE, dtype=jnp.int32))
    blocks = (owners[:, None] * per_device + jnp.arange(per_device, dtype=jnp.int32)[None, :]).reshape(-1)
    counts = jnp.sum(named[:, None, :, :] == blocks[None, :, None, None], axis=3)
    counts = counts + jnp.sum(global_blocks[None, :] == blocks[:, None], axis=1)[None, :, None]
    bias = jnp.where(counts > 0, jnp.log2(counts.astype(jnp.float32)), ABSENT)
    return jnp.repeat(bias, BLK, axis=2)


def body(queries, key_rows, value_rows, window, random_blocks, global_blocks, norm_gain):
    rows, row_width = queries.shape
    head_count = row_width // HD
    shards = lax.axis_size("seq")
    planes = shards // PLANE
    position = lax.axis_index("seq").astype(jnp.int32)
    plane = (position // PLANE).reshape(1)
    bias = count_bias(window, random_blocks, global_blocks, position, shards)
    chunks = min(CHUNKS, head_count)
    width = head_count // chunks * HD
    spans = [slice(c * width, (c + 1) * width) for c in range(chunks)]
    own_queries = [queries[:, span] for span in spans]
    own_pairs = [jnp.stack([key_rows[:, span], value_rows[:, span]]) for span in spans]
    ups, downs = [[q] for q in own_queries], [[q] for q in own_queries]
    pairs = [None] * chunks
    for hop in range(1, planes):
        for c in range(chunks):
            up = along(ups[c][-1], shards, 1, hop - 1, planes - 1)
            down = along(downs[c][-1], shards, -1, 1, planes - hop + 1)
            if hop == 1:
                pairs[c] = [own_pairs[c], exchange(own_pairs[c], shards, 1), exchange(own_pairs[c], shards, 2)]
            up, down = lax.optimization_barrier((up, down))
            if hop == min(2, planes - 1):
                up, down, *pairs[c][1:] = lax.optimization_barrier((up, down, *pairs[c][1:]))
                relay, flip = (pairs[c][1], 2) if c % 2 == 0 else (pairs[c][2], 1)
                pairs[c].append(exchange(relay, shards, flip))
            ups[c].append(up)
            downs[c].append(down)
    heads = width // HD
    parts = [attention(plane, bias, own_queries[c], ups[c][1:], downs[c][1:], pairs[c]) for c in range(chunks)]
    up_runs, down_runs = [None] * chunks, [None] * chunks
    for step in range(1, planes):
        for c in range(chunks):
            up, down = parts[c][planes - step - 1], parts[c][step - 1]
            if step > 1:
                up, down = merged(plane, planes, heads, up, up_runs[c], down, down_runs[c])
            up = along(up, shards, 1, 0, step)
            down = along(down, shards, -1, planes - step, planes)
            up_runs[c], down_runs[c] = lax.optimization_barrier((up, down))
    gain = norm_gain.reshape(1, row_width)
    attended, squares = [], 0.0
    for c in range(chunks):
        own, own_lse = parts[c][-2:]
        rows_c, squares_c = finished(
            plane, planes, heads, own, own_lse, up_runs[c], down_runs[c], gain[:, spans[c]]
        )
        attended.append(rows_c)
        squares = squares + squares_c
    all_squares = lax.psum(squares.reshape(-1), "head")
    inverse = lax.rsqrt(all_squares / D + 1e-06)
    return (jnp.concatenate(attended, axis=1) * inverse[:, None]).astype(jnp.bfloat16)


def solution(mesh):
    placed = (
        P("seq", "head"),
        P("seq", "head"),
        P("seq", "head"),
        P("seq", None),
        P("seq", None),
        P(),
        P("head"),
    )
    return jax.shard_map(
        body, mesh=mesh, in_specs=placed, out_specs=P("seq", "head"), check_vma=False
    )
```

```python
from functools import partial
import math

import jax
import jax.numpy as jnp
from jax import lax
from jax.experimental import pallas as pl
from jax.experimental.pallas import tpu as pltpu
from jax.sharding import PartitionSpec as P

HD = 128
D = 4096
BLK = 64
PLANE = 4
GROUP = 8
SHARES = (1, 2)
TIES = ((1, 1), (1, 1), 0, 1)
SPLIT = True
COST = 8
TIEOWN = (3, 0)
TIES0 = 0
ABSENT = -1e30
NOTHING = 1e-30
VMEM = 40 * 2**20
BIG = 40 * 2**20
SPACE = pltpu.HBM


def up_to(rows, multiple):
    return -(-rows // multiple) * multiple


def exchange(array, shards, flip):
    return lax.ppermute(array, "seq", [(i, i ^ flip) for i in range(shards)])


def along(array, shards, step, first, last):
    pairs = [(z * PLANE + c, (z + step) * PLANE + c) for z in range(first, last) for c in range(PLANE)]
    return lax.ppermute(array, "seq", pairs)


def split_lse(lse):
    high = lse.astype(jnp.bfloat16).astype(jnp.float32)
    rest = lse - high
    middle = rest.astype(jnp.bfloat16).astype(jnp.float32)
    low = rest - middle
    return jnp.concatenate([high, middle, low, jnp.zeros_like(low)], axis=0).astype(jnp.bfloat16)


def join_lse(packed):
    rows = packed.shape[0] // 4
    pieces = packed.astype(jnp.float32)
    return pieces[:rows] + pieces[rows : 2 * rows] + pieces[2 * rows : 3 * rows]


def chain_sources(order, plane, ups, downs):
    low, even = plane < 2, plane % 2 == 0
    if order == 1:
        return ((plane == 0, downs[3]), (plane == 1, downs[1]), (plane == 2, ups[1]), (plane == 3, ups[3]))
    if order == 2:
        return ((low, downs[2]), (jnp.logical_not(low), ups[2]))
    return ((even, downs[1]), (jnp.logical_not(even), ups[1]))


def attend(planes, orders, heads, group, chained, stacked, table_ref, bias_ref, *refs):
    names = iter(refs)
    own = next(names)
    sources = [own] + [next(names) for _ in range(2 * (planes - 1) if chained else planes - 1)]
    ups, downs = sources[:planes], [own] + sources[planes:]
    if stacked:
        pairs = [(ref.at[0], ref.at[1]) for ref in (next(names) for _ in range(PLANE))]
    else:
        pairs = [(next(names), next(names)) for _ in range(PLANE)]
    sent = [order for order in orders if order]
    outs = {order: next(names) for order in sent}
    if 0 in orders:
        own_ref, own_lse_ref = next(names), next(names)
    query_ref, pair_ref, lse_ref, query_sem, pair_sem = names
    plane = table_ref[0]
    rows = own.shape[0]
    blocks = PLANE * rows // BLK
    batch = blocks // PLANE
    lanes = group * HD
    steps = heads // group
    scale = HD**-0.5 * math.log2(math.e)

    def pair_copy(step, j, half):
        at = pl.ds(pl.multiple_of(step * lanes, lanes), lanes)
        return pltpu.make_async_copy(
            pairs[j][half].at[:, at], pair_ref.at[half, pl.ds(j * rows, rows), at], pair_sem.at[step, j, half]
        )

    def query_copy(step, n, source):
        at = pl.ds(pl.multiple_of(step * lanes, lanes), lanes)
        return pltpu.make_async_copy(source.at[pl.ds(0, rows), at], query_ref.at[n, :, at], query_sem.at[step, n])

    for step in range(steps):
        for n, order in enumerate(orders):
            if order == 0 or not chained:
                query_copy(step, n, sources[order]).start()
            else:
                for holds, source in chain_sources(order, plane, ups, downs):
                    pl.when(holds)(query_copy(step, n, source).start)
        for j in range(PLANE):
            for half in range(2):
                pair_copy(step, j, half).start()

    def one_step(step, carry):
        for n in range(len(orders)):
            query_copy(step, n, own).wait()
        for j in range(PLANE):
            for half in range(2):
                pair_copy(step, j, half).wait()
        at = pl.ds(pl.multiple_of(step * lanes, lanes), lanes)
        for n, order in enumerate(orders):
            query = query_ref[n, :, at]
            count = table_ref[1 + order]

            def batch_scores(i):
                start = 1 + planes + order * blocks + i * batch
                spots = [pl.ds(pl.multiple_of(table_ref[start + b] * BLK, BLK), BLK) for b in range(batch)]
                keys = jnp.concatenate([pair_ref[0, spot, at] for spot in spots], axis=0)
                values = jnp.concatenate([pair_ref[1, spot, at] for spot in spots], axis=0)
                bias = bias_ref[order * PLANE + i][:batch]
                scores = []
                for h in range(group):
                    of = slice(h * HD, (h + 1) * HD)
                    product = lax.dot_general(
                        keys[:, of], query[:, of], (((1,), (1,)), ((), ())), preferred_element_type=jnp.float32
                    )
                    scores.append(product.reshape(batch, BLK, rows))
                return scores, bias, values

            def highest(scores, bias):
                top = jnp.max(scores.reshape(batch, BLK // 8, 8, rows), axis=1) * scale + bias[:, None, :]
                return jnp.max(jnp.max(top, axis=0), axis=0, keepdims=True)

            def weigh(scores, bias, peak, values, h):
                weight = jnp.exp2(scores * scale - (peak - bias)[:, None, :])
                total = jnp.sum(weight.reshape(batch * BLK, rows), axis=0, keepdims=True)
                part = lax.dot_general(
                    values[:, h * HD : (h + 1) * HD],
                    weight.astype(jnp.bfloat16).reshape(batch * BLK, rows),
                    (((0,), (0,)), ((), ())),
                    preferred_element_type=jnp.float32,
                )
                return total, part

            def first():
                scores, bias, values = batch_scores(0)
                state = []
                for h in range(group):
                    peak = jnp.maximum(highest(scores[h], bias), ABSENT / 2)
                    state.append((peak, *weigh(scores[h], bias, peak, values, h)))
                return tuple(state)

            def more(i, state):
                scores, bias, values = batch_scores(i)
                after = []
                for h in range(group):
                    peak, total, part = state[h]
                    higher = jnp.maximum(peak, highest(scores[h], bias))
                    shrink = jnp.exp2(peak - higher)
                    added, extra = weigh(scores[h], bias, higher, values, h)
                    after.append((higher, total * shrink + added, part * shrink + extra))
                return tuple(after)

            state = lax.fori_loop(1, count, more, first())
            for h in range(group):
                peak, total, part = state[h]
                total = jnp.maximum(total, NOTHING)
                head = step * group + h
                part = part * (1.0 / total)
                lse_ref[n, pl.ds(head, 1), :] = peak + jnp.log2(total)
                to = pl.ds(pl.multiple_of(head * HD, HD), HD)
                if order == 0:
                    own_ref[to, :] = part
                else:
                    outs[order][to, :] = part.astype(jnp.bfloat16)
        return carry

    lax.fori_loop(0, steps, one_step, 0)
    for n, order in enumerate(orders):
        if order == 0:
            own_lse_ref[...] = lse_ref[n]
        else:
            outs[order][heads * HD :, :] = split_lse(lse_ref[n])


def attention(name, orders, table, bias, own, arrived, pairs):
    rows, width = own.shape
    heads, planes = width // HD, bias.shape[0] // PLANE
    chained, stacked = len(arrived) > planes - 1, len(pairs) == PLANE
    group = math.gcd(heads, GROUP)
    lse_rows = up_to(heads, 8)
    anywhere, whole = pl.BlockSpec(memory_space=SPACE), pl.BlockSpec(memory_space=pltpu.VMEM)
    message = jax.ShapeDtypeStruct((width + 4 * lse_rows, rows), jnp.bfloat16)
    outs = [message for order in orders if order]
    if 0 in orders:
        outs += [jax.ShapeDtypeStruct((width, rows), jnp.float32), jax.ShapeDtypeStruct((lse_rows, rows), jnp.float32)]
    products = heads * len(orders) * PLANE * rows * rows // 2
    return pl.pallas_call(
        partial(attend, planes, orders, heads, group, chained, stacked),
        out_shape=outs,
        in_specs=[pl.BlockSpec(memory_space=pltpu.SMEM), whole] + [anywhere] * (1 + len(arrived) + len(pairs)),
        out_specs=[whole] * len(outs),
        scratch_shapes=[
            pltpu.VMEM((len(orders), rows, width), jnp.bfloat16),
            pltpu.VMEM((2, PLANE * rows, width), jnp.bfloat16),
            pltpu.VMEM((len(orders), lse_rows, rows), jnp.float32),
            pltpu.SemaphoreType.DMA((heads // group, len(orders))),
            pltpu.SemaphoreType.DMA((heads // group, PLANE, 2)),
        ],
        cost_estimate=pl.CostEstimate(
            flops=4 * products * HD, bytes_accessed=COST * 2**20, transcendentals=products
        ),
        compiler_params=pltpu.CompilerParams(vmem_limit_bytes=BIG),
        name=name,
    )(table, bias, own, *arrived, *pairs)


def merge(planes, heads, plane_ref, one_ref, other_ref, up_ref, down_ref, up_out, down_out):
    plane = plane_ref[0]

    def merge_into(mine, came, out, valid):
        mine_lse = join_lse(mine[heads * HD :, :])
        came_lse = jnp.where(valid, join_lse(came[heads * HD :, :]), ABSENT)
        peak = jnp.maximum(mine_lse, came_lse)
        mine_weight, came_weight = jnp.exp2(mine_lse - peak), jnp.exp2(came_lse - peak)
        total = mine_weight + came_weight
        mine_weight, came_weight = mine_weight / total, came_weight / total
        for head in range(heads):
            at = slice(head * HD, (head + 1) * HD)
            mixed = mine[at, :].astype(jnp.float32) * mine_weight[head : head + 1]
            mixed += came[at, :].astype(jnp.float32) * came_weight[head : head + 1]
            out[at, :] = mixed.astype(jnp.bfloat16)
        out[heads * HD :, :] = split_lse(peak + jnp.log2(total))

    @pl.when(plane % 2 == 0)
    def _():
        merge_into(one_ref, up_ref, up_out, plane > 0)
        merge_into(other_ref, down_ref, down_out, plane < planes - 1)

    @pl.when(plane % 2 == 1)
    def _():
        merge_into(other_ref, up_ref, up_out, plane > 0)
        merge_into(one_ref, down_ref, down_out, plane < planes - 1)


def merged(plane, planes, heads, *messages):
    spec = pl.BlockSpec(memory_space=pltpu.VMEM)
    size = math.prod(messages[0].shape)
    return pl.pallas_call(
        partial(merge, planes, heads),
        out_shape=[jax.ShapeDtypeStruct(messages[0].shape, jnp.bfloat16)] * 2,
        in_specs=[pl.BlockSpec(memory_space=pltpu.SMEM)] + [spec] * 4,
        out_specs=[spec] * 2,
        cost_estimate=pl.CostEstimate(flops=8 * size, bytes_accessed=12 * size, transcendentals=0),
        compiler_params=pltpu.CompilerParams(vmem_limit_bytes=VMEM),
        name="merge",
    )(plane, *messages)


def finish(planes, heads, chained, plane_ref, own_ref, own_lse_ref, gain_ref, *refs):
    messages, (out_ref, squares_ref) = refs[:-2], refs[-2:]
    plane = plane_ref[0]
    lses = [own_lse_ref[...]] + [join_lse(message[heads * HD :, :]) for message in messages]
    if chained:
        lses[1] = jnp.where(plane > 0, lses[1], ABSENT)
        lses[2] = jnp.where(plane < planes - 1, lses[2], ABSENT)
    peak = lses[0]
    for lse in lses[1:]:
        peak = jnp.maximum(peak, lse)
    weights = [jnp.exp2(lse - peak) for lse in lses]
    total = sum(weights[1:], weights[0])
    weights = [weight / total for weight in weights]
    squares = 0.0
    for head in range(heads):
        at = slice(head * HD, (head + 1) * HD)
        row = slice(head, head + 1)
        mixed = own_ref[at, :] * weights[0][row]
        for message, weight in zip(messages, weights[1:]):
            mixed += message[at, :].astype(jnp.float32) * weight[row]
        squares += jnp.sum(mixed * mixed, axis=0, keepdims=True)
        out_ref[:, at] = mixed.T * gain_ref[:, at]
    squares_ref[...] = squares


def finished(plane, planes, heads, chained, own, own_lse, gain, messages):
    spec = pl.BlockSpec(memory_space=pltpu.VMEM)
    width, rows = own.shape
    return pl.pallas_call(
        partial(finish, planes, heads, chained),
        out_shape=[
            jax.ShapeDtypeStruct((rows, width), jnp.float32),
            jax.ShapeDtypeStruct((1, rows), jnp.float32),
        ],
        in_specs=[pl.BlockSpec(memory_space=pltpu.SMEM)] + [spec] * (3 + len(messages)),
        out_specs=[spec] * 2,
        cost_estimate=pl.CostEstimate(flops=8 * own.size, bytes_accessed=12 * own.size, transcendentals=0),
        compiler_params=pltpu.CompilerParams(vmem_limit_bytes=VMEM),
        name="finish",
    )(plane, own, own_lse, gain, *messages)


def tables(named, global_blocks, plane, corner, planes):
    per_device = named.shape[1]
    count = PLANE * per_device
    owners = plane * PLANE + (corner ^ jnp.arange(PLANE, dtype=jnp.int32))
    blocks = (owners[:, None] * per_device + jnp.arange(per_device, dtype=jnp.int32)[None, :]).reshape(-1)
    times = jnp.sum(named[:, None, :, :] == blocks[None, :, None, None], axis=3)
    times = times + jnp.sum(global_blocks[None, :] == blocks[:, None], axis=1)[None, :, None]
    needed = jnp.max(times, axis=2) > 0
    earlier = jnp.arange(count)[:, None] < jnp.arange(count)[None, :]
    place = jnp.sum(needed[:, :, None] & earlier[None], axis=1)
    chosen = needed[:, None, :] & (place[:, None, :] == jnp.arange(count)[None, :, None])
    spots = jnp.sum(jnp.where(chosen, jnp.arange(count)[None, None, :], 0), axis=2)
    times = jnp.sum(jnp.where(chosen[:, :, :, None], times[:, None, :, :], 0), axis=2)
    bias = jnp.where(times > 0, jnp.log2(times.astype(jnp.float32)), ABSENT)
    bias = jnp.repeat(bias, BLK, axis=2).reshape(planes * PLANE, per_device, per_device * BLK)
    bias = jnp.pad(bias, ((0, 0), (0, up_to(per_device, 8) - per_device), (0, 0)))
    batches = jnp.maximum(-(-jnp.sum(needed, axis=1) // per_device), 1)
    table = jnp.concatenate([plane.reshape(1), batches, spots.reshape(-1)]).astype(jnp.int32)
    return table, bias


def flipped(array, shards, flip):
    return exchange(array, shards, flip * PLANE)


tie = lax.optimization_barrier


def travel(owns, keys, values, own_named, shards, plane):
    planes = shards // PLANE
    arrived, pairs = [], []
    for own, key, value in zip(owns, keys, values):
        arrived.append([flipped(own, shards, planes - order) for order in range(1, planes)])
        pairs.append([exchange(half, shards, flip) if flip else half for flip in range(PLANE) for half in (key, value)])
    return arrived, pairs, [flipped(own_named, shards, planes - order) for order in range(1, planes)]


def travel_on_line(owns, keys, values, own_named, shards, plane):
    groups = range(len(owns))
    ups, downs, near, far, diagonal = ([[] for _ in groups] for _ in range(5))
    rows, width = owns[0].shape
    blocks, names = own_named.shape
    note = jnp.pad(own_named.astype(owns[0].dtype), ((0, up_to(blocks, 16) - blocks), (0, width - names)))
    owns = [jnp.concatenate([owns[0], note], axis=0), *owns[1:]]
    for hop in range(1, 4):
        for c in groups:
            up, down = (ups[c][-1], downs[c][-1]) if hop > 1 else (owns[c], owns[c])
            key, value = keys[c], values[c]
            if hop == 2:
                up, down, *first = tie((up, down, near[c][0], far[c][1]) if TIES[0][c] else (up, down))
                near[c][0], far[c][1] = first or (near[c][0], far[c][1])
            if hop == 3:
                up, down, *second = tie((up, down, near[c][1], far[c][0]) if TIES[1][c] else (up, down))
                near[c][1], far[c][0] = second or (near[c][1], far[c][0])
            up, down = along(up, shards, 1, hop - 1, 3), along(down, shards, -1, 1, 5 - hop)
            if hop == 1:
                if c and TIES[2]:
                    key, value, *_ = tie((key, value, near[c - 1][1], far[c - 1][0]))
                elif c and TIES[3]:
                    key, value, *_ = tie((key, value, near[c - 1][0], far[c - 1][1]))
                near[c] = [exchange(key, shards, 1), exchange(value, shards, 1)]
                far[c] = [exchange(key, shards, 2), exchange(value, shards, 2)]
            up, down = tie((up, down))
            if hop == 2:
                diagonal[c] = [exchange(near[c][0], shards, 2), exchange(far[c][1], shards, 1)]
            ups[c].append(up)
            downs[c].append(down)
    arrived = [[*ups[c], *downs[c]] for c in groups]
    ups, downs = ([array[rows : rows + blocks, :names] for array in arrays] for arrays in (ups[0], downs[0]))
    named = [jnp.zeros_like(ups[0])] * 3
    for order in range(1, 4):
        for holds, array in chain_sources(order, plane, [None, *ups], [None, *downs]):
            named[order - 1] = jnp.where(holds, array, named[order - 1])
    named = [name.astype(own_named.dtype) for name in named]
    pairs = [[keys[c], values[c], *near[c], *far[c], *diagonal[c]] for c in groups]
    return arrived, pairs, named


def body(queries, key_rows, value_rows, window, random_blocks, global_blocks, norm_gain):
    rows, row_width = queries.shape
    head_count = row_width // HD
    shards = lax.axis_size("seq")
    planes = shards // PLANE
    line = planes == 4
    position = lax.axis_index("seq").astype(jnp.int32)
    plane, corner = position // PLANE, position % PLANE
    own_named = jnp.concatenate([window, random_blocks], axis=1)
    bounds = [0] + [head_count * share // SHARES[-1] * HD for share in SHARES]
    spans = [slice(low, high) for low, high in zip(bounds[:-1], bounds[1:])]
    owns, keys, values = ([array[:, span] for span in spans] for array in (queries, key_rows, value_rows))
    arrived, pairs, named = (travel_on_line if line else travel)(owns, keys, values, own_named, shards, plane)
    table, bias = tables(jnp.stack([own_named, *named]), global_blocks, plane, corner, planes)
    plane = plane.reshape(1)
    gain = norm_gain.reshape(1, row_width)
    parts, own_parts = [], []
    for own, came, pair in zip(owns, arrived, pairs):
        given = table, bias, own, came, pair
        if SPLIT:
            if TIES0:
                own_part, own_lse = attention("own_part", (0,), *given)
                given = (*given[:2], *tie((given[2], own_lse))[:1], *given[3:])
            sent = attention("sent_parts", tuple(range(1, planes)), *given)
            if not TIES0:
                own_part, own_lse = attention("own_part", (0,), *given)
        else:
            sent = attention("far_part", (1,), *given)
            *rest, own_part, own_lse = attention("near_parts", (*range(2, planes), 0), *given)
            sent = [*sent, *rest]
        parts.append([None, *sent])
        own_parts.append((own_part, own_lse))
    heads = [(span.stop - span.start) // HD for span in spans]
    runs = [None] * len(spans)
    for step in range(1, planes):
        for c in range(len(spans)):
            if line:
                up = down = parts[c][step]
                if step > 1:
                    up, down = merged(plane, planes, heads[c], up, parts[c][planes - step], *runs[c])
                if step == TIEOWN[c]:
                    up, down, *own_parts[c] = tie((up, down, *own_parts[c]))
                runs[c] = tie((along(up, shards, 1, 0, step), along(down, shards, -1, planes - step, planes)))
            elif step == 1:
                runs[c] = [flipped(parts[c][order], shards, planes - order) for order in range(1, planes)]
    attended, squares = [], 0.0
    for c, span in enumerate(spans):
        rows_c, squares_c = finished(plane, planes, heads[c], line, *own_parts[c], gain[:, span], runs[c])
        attended.append(rows_c)
        squares = squares + squares_c
    all_squares = lax.psum(squares.reshape(-1), "head")
    inverse = lax.rsqrt(all_squares / D + 1e-06)
    return (jnp.concatenate(attended, axis=1) * inverse[:, None]).astype(jnp.bfloat16)


def solution(mesh):
    placed = (
        P("seq", "head"),
        P("seq", "head"),
        P("seq", "head"),
        P("seq", None),
        P("seq", None),
        P(),
        P("head"),
    )
    return jax.shard_map(
        body, mesh=mesh, in_specs=placed, out_specs=P("seq", "head"), check_vma=False
    )
```

```python
from functools import partial
import math

import jax
import jax.numpy as jnp
from jax import lax
from jax.experimental import pallas as pl
from jax.experimental.pallas import tpu as pltpu
from jax.sharding import PartitionSpec as P

HD = 128
D = 4096
BLK = 64
PLANE = 4
GROUP = 8
SHARES = (1, 2)
TIES = ((1, 1), (1, 1), 0, 1)
SPLIT = ((1,), (2, 3), (0,))
TIEOWN = (3, 0)
ABSENT = -1e30
NOTHING = 1e-30
VMEM = 40 * 2**20
BIG = 40 * 2**20
SPACE = pltpu.HBM


def up_to(rows, multiple):
    return -(-rows // multiple) * multiple


def exchange(array, shards, flip):
    return lax.ppermute(array, "seq", [(i, i ^ flip) for i in range(shards)])


def along(array, shards, step, first, last):
    pairs = [(z * PLANE + c, (z + step) * PLANE + c) for z in range(first, last) for c in range(PLANE)]
    return lax.ppermute(array, "seq", pairs)


def split_lse(lse):
    high = lse.astype(jnp.bfloat16).astype(jnp.float32)
    rest = lse - high
    middle = rest.astype(jnp.bfloat16).astype(jnp.float32)
    low = rest - middle
    return jnp.concatenate([high, middle, low, jnp.zeros_like(low)], axis=0).astype(jnp.bfloat16)


def join_lse(packed):
    rows = packed.shape[0] // 4
    pieces = packed.astype(jnp.float32)
    return pieces[:rows] + pieces[rows : 2 * rows] + pieces[2 * rows : 3 * rows]


def chain_sources(order, plane, ups, downs):
    low, even = plane < 2, plane % 2 == 0
    if order == 1:
        return ((plane == 0, downs[3]), (plane == 1, downs[1]), (plane == 2, ups[1]), (plane == 3, ups[3]))
    if order == 2:
        return ((low, downs[2]), (jnp.logical_not(low), ups[2]))
    return ((even, downs[1]), (jnp.logical_not(even), ups[1]))


def attend(planes, orders, heads, group, chained, stacked, table_ref, bias_ref, *refs):
    names = iter(refs)
    own = next(names)
    sources = [own] + [next(names) for _ in range(2 * (planes - 1) if chained else planes - 1)]
    ups, downs = sources[:planes], [own] + sources[planes:]
    if stacked:
        pairs = [(ref.at[0], ref.at[1]) for ref in (next(names) for _ in range(PLANE))]
    else:
        pairs = [(next(names), next(names)) for _ in range(PLANE)]
    sent = [order for order in orders if order]
    outs = {order: next(names) for order in sent}
    if 0 in orders:
        own_ref, own_lse_ref = next(names), next(names)
    query_ref, pair_ref, lse_ref, query_sem, pair_sem = names
    plane = table_ref[0]
    rows = own.shape[0]
    blocks = PLANE * rows // BLK
    batch = blocks // PLANE
    lanes = group * HD
    steps = heads // group
    scale = HD**-0.5 * math.log2(math.e)

    def pair_copy(step, j, half):
        at = pl.ds(pl.multiple_of(step * lanes, lanes), lanes)
        return pltpu.make_async_copy(
            pairs[j][half].at[:, at], pair_ref.at[half, pl.ds(j * rows, rows), at], pair_sem.at[step, j, half]
        )

    def query_copy(step, n, source):
        at = pl.ds(pl.multiple_of(step * lanes, lanes), lanes)
        return pltpu.make_async_copy(source.at[pl.ds(0, rows), at], query_ref.at[n, :, at], query_sem.at[step, n])

    for step in range(steps):
        for n, order in enumerate(orders):
            if order == 0 or not chained:
                query_copy(step, n, sources[order]).start()
            else:
                for holds, source in chain_sources(order, plane, ups, downs):
                    pl.when(holds)(query_copy(step, n, source).start)
        for j in range(PLANE):
            for half in range(2):
                pair_copy(step, j, half).start()

    def one_step(step, carry):
        for n in range(len(orders)):
            query_copy(step, n, own).wait()
        for j in range(PLANE):
            for half in range(2):
                pair_copy(step, j, half).wait()
        at = pl.ds(pl.multiple_of(step * lanes, lanes), lanes)
        for n, order in enumerate(orders):
            query = query_ref[n, :, at]
            count = table_ref[1 + order]

            def batch_scores(i):
                start = 1 + planes + order * blocks + i * batch
                spots = [pl.ds(pl.multiple_of(table_ref[start + b] * BLK, BLK), BLK) for b in range(batch)]
                keys = jnp.concatenate([pair_ref[0, spot, at] for spot in spots], axis=0)
                values = jnp.concatenate([pair_ref[1, spot, at] for spot in spots], axis=0)
                bias = bias_ref[order * PLANE + i][:batch]
                scores = []
                for h in range(group):
                    of = slice(h * HD, (h + 1) * HD)
                    product = lax.dot_general(
                        keys[:, of], query[:, of], (((1,), (1,)), ((), ())), preferred_element_type=jnp.float32
                    )
                    scores.append(product.reshape(batch, BLK, rows))
                return scores, bias, values

            def highest(scores, bias):
                top = jnp.max(scores.reshape(batch, BLK // 8, 8, rows), axis=1) * scale + bias[:, None, :]
                return jnp.max(jnp.max(top, axis=0), axis=0, keepdims=True)

            def weigh(scores, bias, peak, values, h):
                weight = jnp.exp2(scores * scale - (peak - bias)[:, None, :])
                total = jnp.sum(weight.reshape(batch * BLK, rows), axis=0, keepdims=True)
                part = lax.dot_general(
                    values[:, h * HD : (h + 1) * HD],
                    weight.astype(jnp.bfloat16).reshape(batch * BLK, rows),
                    (((0,), (0,)), ((), ())),
                    preferred_element_type=jnp.float32,
                )
                return total, part

            def first():
                scores, bias, values = batch_scores(0)
                state = []
                for h in range(group):
                    peak = jnp.maximum(highest(scores[h], bias), ABSENT / 2)
                    state.append((peak, *weigh(scores[h], bias, peak, values, h)))
                return tuple(state)

            def more(i, state):
                scores, bias, values = batch_scores(i)
                after = []
                for h in range(group):
                    peak, total, part = state[h]
                    higher = jnp.maximum(peak, highest(scores[h], bias))
                    shrink = jnp.exp2(peak - higher)
                    added, extra = weigh(scores[h], bias, higher, values, h)
                    after.append((higher, total * shrink + added, part * shrink + extra))
                return tuple(after)

            state = lax.fori_loop(1, count, more, first())
            for h in range(group):
                peak, total, part = state[h]
                total = jnp.maximum(total, NOTHING)
                head = step * group + h
                part = part * (1.0 / total)
                lse_ref[n, pl.ds(head, 1), :] = peak + jnp.log2(total)
                to = pl.ds(pl.multiple_of(head * HD, HD), HD)
                if order == 0:
                    own_ref[to, :] = part
                else:
                    outs[order][to, :] = part.astype(jnp.bfloat16)
        return carry

    lax.fori_loop(0, steps, one_step, 0)
    for n, order in enumerate(orders):
        if order == 0:
            own_lse_ref[...] = lse_ref[n]
        else:
            outs[order][heads * HD :, :] = split_lse(lse_ref[n])


def attention(name, orders, table, bias, own, arrived, pairs):
    rows, width = own.shape
    heads, planes = width // HD, bias.shape[0] // PLANE
    chained, stacked = len(arrived) > planes - 1, len(pairs) == PLANE
    group = math.gcd(heads, GROUP)
    lse_rows = up_to(heads, 8)
    anywhere, whole = pl.BlockSpec(memory_space=SPACE), pl.BlockSpec(memory_space=pltpu.VMEM)
    message = jax.ShapeDtypeStruct((width + 4 * lse_rows, rows), jnp.bfloat16)
    outs = [message for order in orders if order]
    if 0 in orders:
        outs += [jax.ShapeDtypeStruct((width, rows), jnp.float32), jax.ShapeDtypeStruct((lse_rows, rows), jnp.float32)]
    products = heads * len(orders) * PLANE * rows * rows // 2
    return pl.pallas_call(
        partial(attend, planes, orders, heads, group, chained, stacked),
        out_shape=outs,
        in_specs=[pl.BlockSpec(memory_space=pltpu.SMEM), whole] + [anywhere] * (1 + len(arrived) + len(pairs)),
        out_specs=[whole] * len(outs),
        scratch_shapes=[
            pltpu.VMEM((len(orders), rows, width), jnp.bfloat16),
            pltpu.VMEM((2, PLANE * rows, width), jnp.bfloat16),
            pltpu.VMEM((len(orders), lse_rows, rows), jnp.float32),
            pltpu.SemaphoreType.DMA((heads // group, len(orders))),
            pltpu.SemaphoreType.DMA((heads // group, PLANE, 2)),
        ],
        cost_estimate=pl.CostEstimate(
            flops=4 * products * HD, bytes_accessed=8 * 2**20, transcendentals=products
        ),
        compiler_params=pltpu.CompilerParams(vmem_limit_bytes=BIG),
        name=name,
    )(table, bias, own, *arrived, *pairs)


def merge(planes, heads, plane_ref, one_ref, other_ref, up_ref, down_ref, up_out, down_out):
    plane = plane_ref[0]

    def merge_into(mine, came, out, valid):
        mine_lse = join_lse(mine[heads * HD :, :])
        came_lse = jnp.where(valid, join_lse(came[heads * HD :, :]), ABSENT)
        peak = jnp.maximum(mine_lse, came_lse)
        mine_weight, came_weight = jnp.exp2(mine_lse - peak), jnp.exp2(came_lse - peak)
        total = mine_weight + came_weight
        mine_weight, came_weight = mine_weight / total, came_weight / total
        for head in range(heads):
            at = slice(head * HD, (head + 1) * HD)
            mixed = mine[at, :].astype(jnp.float32) * mine_weight[head : head + 1]
            mixed += came[at, :].astype(jnp.float32) * came_weight[head : head + 1]
            out[at, :] = mixed.astype(jnp.bfloat16)
        out[heads * HD :, :] = split_lse(peak + jnp.log2(total))

    @pl.when(plane % 2 == 0)
    def _():
        merge_into(one_ref, up_ref, up_out, plane > 0)
        merge_into(other_ref, down_ref, down_out, plane < planes - 1)

    @pl.when(plane % 2 == 1)
    def _():
        merge_into(other_ref, up_ref, up_out, plane > 0)
        merge_into(one_ref, down_ref, down_out, plane < planes - 1)


def merged(plane, planes, heads, *messages):
    spec = pl.BlockSpec(memory_space=pltpu.VMEM)
    size = math.prod(messages[0].shape)
    return pl.pallas_call(
        partial(merge, planes, heads),
        out_shape=[jax.ShapeDtypeStruct(messages[0].shape, jnp.bfloat16)] * 2,
        in_specs=[pl.BlockSpec(memory_space=pltpu.SMEM)] + [spec] * 4,
        out_specs=[spec] * 2,
        cost_estimate=pl.CostEstimate(flops=8 * size, bytes_accessed=12 * size, transcendentals=0),
        compiler_params=pltpu.CompilerParams(vmem_limit_bytes=VMEM),
        name="merge",
    )(plane, *messages)


def finish(planes, heads, chained, plane_ref, own_ref, own_lse_ref, gain_ref, *refs):
    messages, (out_ref, squares_ref) = refs[:-2], refs[-2:]
    plane = plane_ref[0]
    lses = [own_lse_ref[...]] + [join_lse(message[heads * HD :, :]) for message in messages]
    if chained:
        lses[1] = jnp.where(plane > 0, lses[1], ABSENT)
        lses[2] = jnp.where(plane < planes - 1, lses[2], ABSENT)
    peak = lses[0]
    for lse in lses[1:]:
        peak = jnp.maximum(peak, lse)
    weights = [jnp.exp2(lse - peak) for lse in lses]
    total = sum(weights[1:], weights[0])
    weights = [weight / total for weight in weights]
    squares = 0.0
    for head in range(heads):
        at = slice(head * HD, (head + 1) * HD)
        row = slice(head, head + 1)
        mixed = own_ref[at, :] * weights[0][row]
        for message, weight in zip(messages, weights[1:]):
            mixed += message[at, :].astype(jnp.float32) * weight[row]
        squares += jnp.sum(mixed * mixed, axis=0, keepdims=True)
        out_ref[:, at] = mixed.T * gain_ref[:, at]
    squares_ref[...] = squares


def finished(plane, planes, heads, chained, own, own_lse, gain, messages):
    spec = pl.BlockSpec(memory_space=pltpu.VMEM)
    width, rows = own.shape
    return pl.pallas_call(
        partial(finish, planes, heads, chained),
        out_shape=[
            jax.ShapeDtypeStruct((rows, width), jnp.float32),
            jax.ShapeDtypeStruct((1, rows), jnp.float32),
        ],
        in_specs=[pl.BlockSpec(memory_space=pltpu.SMEM)] + [spec] * (3 + len(messages)),
        out_specs=[spec] * 2,
        cost_estimate=pl.CostEstimate(flops=8 * own.size, bytes_accessed=12 * own.size, transcendentals=0),
        compiler_params=pltpu.CompilerParams(vmem_limit_bytes=VMEM),
        name="finish",
    )(plane, own, own_lse, gain, *messages)


def tables(named, global_blocks, plane, corner, planes):
    per_device = named.shape[1]
    count = PLANE * per_device
    owners = plane * PLANE + (corner ^ jnp.arange(PLANE, dtype=jnp.int32))
    blocks = (owners[:, None] * per_device + jnp.arange(per_device, dtype=jnp.int32)[None, :]).reshape(-1)
    times = jnp.sum(named[:, None, :, :] == blocks[None, :, None, None], axis=3)
    times = times + jnp.sum(global_blocks[None, :] == blocks[:, None], axis=1)[None, :, None]
    needed = jnp.max(times, axis=2) > 0
    earlier = jnp.arange(count)[:, None] < jnp.arange(count)[None, :]
    place = jnp.sum(needed[:, :, None] & earlier[None], axis=1)
    chosen = needed[:, None, :] & (place[:, None, :] == jnp.arange(count)[None, :, None])
    spots = jnp.sum(jnp.where(chosen, jnp.arange(count)[None, None, :], 0), axis=2)
    times = jnp.sum(jnp.where(chosen[:, :, :, None], times[:, None, :, :], 0), axis=2)
    bias = jnp.where(times > 0, jnp.log2(times.astype(jnp.float32)), ABSENT)
    bias = jnp.repeat(bias, BLK, axis=2).reshape(planes * PLANE, per_device, per_device * BLK)
    bias = jnp.pad(bias, ((0, 0), (0, up_to(per_device, 8) - per_device), (0, 0)))
    batches = jnp.maximum(-(-jnp.sum(needed, axis=1) // per_device), 1)
    table = jnp.concatenate([plane.reshape(1), batches, spots.reshape(-1)]).astype(jnp.int32)
    return table, bias


def flipped(array, shards, flip):
    return exchange(array, shards, flip * PLANE)


tie = lax.optimization_barrier


def travel(owns, keys, values, own_named, shards, plane):
    planes = shards // PLANE
    arrived, pairs = [], []
    for own, key, value in zip(owns, keys, values):
        arrived.append([flipped(own, shards, planes - order) for order in range(1, planes)])
        pairs.append([exchange(half, shards, flip) if flip else half for flip in range(PLANE) for half in (key, value)])
    return arrived, pairs, [flipped(own_named, shards, planes - order) for order in range(1, planes)]


def travel_on_line(owns, keys, values, own_named, shards, plane):
    groups = range(len(owns))
    ups, downs, near, far, diagonal = ([[] for _ in groups] for _ in range(5))
    rows, width = owns[0].shape
    blocks, names = own_named.shape
    note = jnp.pad(own_named.astype(owns[0].dtype), ((0, up_to(blocks, 16) - blocks), (0, width - names)))
    owns = [jnp.concatenate([owns[0], note], axis=0), *owns[1:]]
    for hop in range(1, 4):
        for c in groups:
            up, down = (ups[c][-1], downs[c][-1]) if hop > 1 else (owns[c], owns[c])
            key, value = keys[c], values[c]
            if hop == 2:
                up, down, *first = tie((up, down, near[c][0], far[c][1]) if TIES[0][c] else (up, down))
                near[c][0], far[c][1] = first or (near[c][0], far[c][1])
            if hop == 3:
                up, down, *second = tie((up, down, near[c][1], far[c][0]) if TIES[1][c] else (up, down))
                near[c][1], far[c][0] = second or (near[c][1], far[c][0])
            up, down = along(up, shards, 1, hop - 1, 3), along(down, shards, -1, 1, 5 - hop)
            if hop == 1:
                if c and TIES[2]:
                    key, value, *_ = tie((key, value, near[c - 1][1], far[c - 1][0]))
                elif c and TIES[3]:
                    key, value, *_ = tie((key, value, near[c - 1][0], far[c - 1][1]))
                near[c] = [exchange(key, shards, 1), exchange(value, shards, 1)]
                far[c] = [exchange(key, shards, 2), exchange(value, shards, 2)]
            up, down = tie((up, down))
            if hop == 2:
                diagonal[c] = [exchange(near[c][0], shards, 2), exchange(far[c][1], shards, 1)]
            ups[c].append(up)
            downs[c].append(down)
    arrived = [[*ups[c], *downs[c]] for c in groups]
    ups, downs = ([array[rows : rows + blocks, :names] for array in arrays] for arrays in (ups[0], downs[0]))
    named = [jnp.zeros_like(ups[0])] * 3
    for order in range(1, 4):
        for holds, array in chain_sources(order, plane, [None, *ups], [None, *downs]):
            named[order - 1] = jnp.where(holds, array, named[order - 1])
    named = [name.astype(own_named.dtype) for name in named]
    pairs = [[keys[c], values[c], *near[c], *far[c], *diagonal[c]] for c in groups]
    return arrived, pairs, named


def body(queries, key_rows, value_rows, window, random_blocks, global_blocks, norm_gain):
    rows, row_width = queries.shape
    head_count = row_width // HD
    shards = lax.axis_size("seq")
    planes = shards // PLANE
    line = planes == 4
    position = lax.axis_index("seq").astype(jnp.int32)
    plane, corner = position // PLANE, position % PLANE
    own_named = jnp.concatenate([window, random_blocks], axis=1)
    bounds = [0] + [head_count * share // SHARES[-1] * HD for share in SHARES]
    spans = [slice(low, high) for low, high in zip(bounds[:-1], bounds[1:])]
    owns, keys, values = ([array[:, span] for span in spans] for array in (queries, key_rows, value_rows))
    arrived, pairs, named = (travel_on_line if line else travel)(owns, keys, values, own_named, shards, plane)
    table, bias = tables(jnp.stack([own_named, *named]), global_blocks, plane, corner, planes)
    plane = plane.reshape(1)
    gain = norm_gain.reshape(1, row_width)
    parts, own_parts = [], []
    for own, came, pair in zip(owns, arrived, pairs):
        given = table, bias, own, came, pair
        sent = []
        for orders in SPLIT if line else ((*range(1, planes),), (0,)):
            outs = attention("part", orders, *given)
            if 0 in orders:
                *outs, own_part, own_lse = outs
            sent += outs
        parts.append([None, *sent])
        own_parts.append((own_part, own_lse))
    heads = [(span.stop - span.start) // HD for span in spans]
    runs = [None] * len(spans)
    for step in range(1, planes):
        for c in range(len(spans)):
            if line:
                up = down = parts[c][step]
                if step > 1:
                    up, down = merged(plane, planes, heads[c], up, parts[c][planes - step], *runs[c])
                if step == TIEOWN[c]:
                    up, down, *own_parts[c] = tie((up, down, *own_parts[c]))
                runs[c] = tie((along(up, shards, 1, 0, step), along(down, shards, -1, planes - step, planes)))
            elif step == 1:
                runs[c] = [flipped(parts[c][order], shards, planes - order) for order in range(1, planes)]
    attended, squares = [], 0.0
    for c, span in enumerate(spans):
        rows_c, squares_c = finished(plane, planes, heads[c], line, *own_parts[c], gain[:, span], runs[c])
        attended.append(rows_c)
        squares = squares + squares_c
    all_squares = lax.psum(squares.reshape(-1), "head")
    inverse = lax.rsqrt(all_squares / D + 1e-06)
    return (jnp.concatenate(attended, axis=1) * inverse[:, None]).astype(jnp.bfloat16)


def solution(mesh):
    placed = (
        P("seq", "head"),
        P("seq", "head"),
        P("seq", "head"),
        P("seq", None),
        P("seq", None),
        P(),
        P("head"),
    )
    return jax.shard_map(
        body, mesh=mesh, in_specs=placed, out_specs=P("seq", "head"), check_vma=False
    )
```

```python
from functools import partial
import math

import jax
import jax.numpy as jnp
from jax import lax
from jax.experimental import pallas as pl
from jax.experimental.pallas import tpu as pltpu
from jax.sharding import PartitionSpec as P

HD = 128
D = 4096
BLK = 64
PLANE = 4
GROUP = 8
SHARES = (1, 2)
TIES = ((1, 1), (0, 1), 0, 0)
SPLIT = ((1,), (2, 3), (0,))
TIEOWN = (3, 0)
ABSENT = -1e30
NOTHING = 1e-30
VMEM = 40 * 2**20
BIG = 40 * 2**20
SPACE = pltpu.HBM


def up_to(rows, multiple):
    return -(-rows // multiple) * multiple


def exchange(array, shards, flip):
    return lax.ppermute(array, "seq", [(i, i ^ flip) for i in range(shards)])


def along(array, shards, step, first, last):
    pairs = [(z * PLANE + c, (z + step) * PLANE + c) for z in range(first, last) for c in range(PLANE)]
    return lax.ppermute(array, "seq", pairs)


def split_lse(lse):
    high = lse.astype(jnp.bfloat16).astype(jnp.float32)
    rest = lse - high
    middle = rest.astype(jnp.bfloat16).astype(jnp.float32)
    low = rest - middle
    return jnp.concatenate([high, middle, low, jnp.zeros_like(low)], axis=0).astype(jnp.bfloat16)


def join_lse(packed):
    rows = packed.shape[0] // 4
    pieces = packed.astype(jnp.float32)
    return pieces[:rows] + pieces[rows : 2 * rows] + pieces[2 * rows : 3 * rows]


def chain_sources(order, plane, ups, downs):
    low, even = plane < 2, plane % 2 == 0
    if order == 1:
        return ((plane == 0, downs[3]), (plane == 1, downs[1]), (plane == 2, ups[1]), (plane == 3, ups[3]))
    if order == 2:
        return ((low, downs[2]), (jnp.logical_not(low), ups[2]))
    return ((even, downs[1]), (jnp.logical_not(even), ups[1]))


def attend(planes, orders, heads, group, chained, stacked, table_ref, bias_ref, *refs):
    names = iter(refs)
    own = next(names)
    sources = [own] + [next(names) for _ in range(2 * (planes - 1) if chained else planes - 1)]
    ups, downs = sources[:planes], [own] + sources[planes:]
    if stacked:
        pairs = [(ref.at[0], ref.at[1]) for ref in (next(names) for _ in range(PLANE))]
    else:
        pairs = [(next(names), next(names)) for _ in range(PLANE)]
    sent = [order for order in orders if order]
    outs = {order: next(names) for order in sent}
    if 0 in orders:
        own_ref, own_lse_ref = next(names), next(names)
    query_ref, pair_ref, lse_ref, query_sem, pair_sem = names
    plane = table_ref[0]
    rows = own.shape[0]
    blocks = PLANE * rows // BLK
    batch = blocks // PLANE
    lanes = group * HD
    steps = heads // group
    scale = HD**-0.5 * math.log2(math.e)

    def pair_copy(step, j, half):
        at = pl.ds(pl.multiple_of(step * lanes, lanes), lanes)
        return pltpu.make_async_copy(
            pairs[j][half].at[:, at], pair_ref.at[half, pl.ds(j * rows, rows), at], pair_sem.at[step, j, half]
        )

    def query_copy(step, n, source):
        at = pl.ds(pl.multiple_of(step * lanes, lanes), lanes)
        return pltpu.make_async_copy(source.at[pl.ds(0, rows), at], query_ref.at[n, :, at], query_sem.at[step, n])

    for step in range(steps):
        for n, order in enumerate(orders):
            if order == 0 or not chained:
                query_copy(step, n, sources[order]).start()
            else:
                for holds, source in chain_sources(order, plane, ups, downs):
                    pl.when(holds)(query_copy(step, n, source).start)
        for j in range(PLANE):
            for half in range(2):
                pair_copy(step, j, half).start()

    def one_step(step, carry):
        for n in range(len(orders)):
            query_copy(step, n, own).wait()
        for j in range(PLANE):
            for half in range(2):
                pair_copy(step, j, half).wait()
        at = pl.ds(pl.multiple_of(step * lanes, lanes), lanes)
        for n, order in enumerate(orders):
            query = query_ref[n, :, at]
            count = table_ref[1 + order]

            def batch_scores(i):
                start = 1 + planes + order * blocks + i * batch
                spots = [pl.ds(pl.multiple_of(table_ref[start + b] * BLK, BLK), BLK) for b in range(batch)]
                keys = jnp.concatenate([pair_ref[0, spot, at] for spot in spots], axis=0)
                values = jnp.concatenate([pair_ref[1, spot, at] for spot in spots], axis=0)
                bias = bias_ref[order * PLANE + i][:batch]
                scores = []
                for h in range(group):
                    of = slice(h * HD, (h + 1) * HD)
                    product = lax.dot_general(
                        keys[:, of], query[:, of], (((1,), (1,)), ((), ())), preferred_element_type=jnp.float32
                    )
                    scores.append(product.reshape(batch, BLK, rows))
                return scores, bias, values

            def highest(scores, bias):
                top = jnp.max(scores.reshape(batch, BLK // 8, 8, rows), axis=1) * scale + bias[:, None, :]
                return jnp.max(jnp.max(top, axis=0), axis=0, keepdims=True)

            def weigh(scores, bias, peak, values, h):
                weight = jnp.exp2(scores * scale - (peak - bias)[:, None, :])
                total = jnp.sum(weight.reshape(batch * BLK, rows), axis=0, keepdims=True)
                part = lax.dot_general(
                    values[:, h * HD : (h + 1) * HD],
                    weight.astype(jnp.bfloat16).reshape(batch * BLK, rows),
                    (((0,), (0,)), ((), ())),
                    preferred_element_type=jnp.float32,
                )
                return total, part

            def first():
                scores, bias, values = batch_scores(0)
                state = []
                for h in range(group):
                    peak = jnp.maximum(highest(scores[h], bias), ABSENT / 2)
                    state.append((peak, *weigh(scores[h], bias, peak, values, h)))
                return tuple(state)

            def more(i, state):
                scores, bias, values = batch_scores(i)
                after = []
                for h in range(group):
                    peak, total, part = state[h]
                    higher = jnp.maximum(peak, highest(scores[h], bias))
                    shrink = jnp.exp2(peak - higher)
                    added, extra = weigh(scores[h], bias, higher, values, h)
                    after.append((higher, total * shrink + added, part * shrink + extra))
                return tuple(after)

            state = lax.fori_loop(1, count, more, first())
            for h in range(group):
                peak, total, part = state[h]
                total = jnp.maximum(total, NOTHING)
                head = step * group + h
                part = part * (1.0 / total)
                lse_ref[n, pl.ds(head, 1), :] = peak + jnp.log2(total)
                to = pl.ds(pl.multiple_of(head * HD, HD), HD)
                if order == 0:
                    own_ref[to, :] = part
                else:
                    outs[order][to, :] = part.astype(jnp.bfloat16)
        return carry

    lax.fori_loop(0, steps, one_step, 0)
    for n, order in enumerate(orders):
        if order == 0:
            own_lse_ref[...] = lse_ref[n]
        else:
            outs[order][heads * HD :, :] = split_lse(lse_ref[n])


def attention(name, orders, table, bias, own, arrived, pairs):
    rows, width = own.shape
    heads, planes = width // HD, bias.shape[0] // PLANE
    chained, stacked = len(arrived) > planes - 1, len(pairs) == PLANE
    group = math.gcd(heads, GROUP)
    lse_rows = up_to(heads, 8)
    anywhere, whole = pl.BlockSpec(memory_space=SPACE), pl.BlockSpec(memory_space=pltpu.VMEM)
    message = jax.ShapeDtypeStruct((width + 4 * lse_rows, rows), jnp.bfloat16)
    outs = [message for order in orders if order]
    if 0 in orders:
        outs += [jax.ShapeDtypeStruct((width, rows), jnp.float32), jax.ShapeDtypeStruct((lse_rows, rows), jnp.float32)]
    products = heads * len(orders) * PLANE * rows * rows // 2
    return pl.pallas_call(
        partial(attend, planes, orders, heads, group, chained, stacked),
        out_shape=outs,
        in_specs=[pl.BlockSpec(memory_space=pltpu.SMEM), whole] + [anywhere] * (1 + len(arrived) + len(pairs)),
        out_specs=[whole] * len(outs),
        scratch_shapes=[
            pltpu.VMEM((len(orders), rows, width), jnp.bfloat16),
            pltpu.VMEM((2, PLANE * rows, width), jnp.bfloat16),
            pltpu.VMEM((len(orders), lse_rows, rows), jnp.float32),
            pltpu.SemaphoreType.DMA((heads // group, len(orders))),
            pltpu.SemaphoreType.DMA((heads // group, PLANE, 2)),
        ],
        cost_estimate=pl.CostEstimate(
            flops=4 * products * HD, bytes_accessed=8 * 2**20, transcendentals=products
        ),
        compiler_params=pltpu.CompilerParams(vmem_limit_bytes=BIG),
        name=name,
    )(table, bias, own, *arrived, *pairs)


def merge(planes, heads, plane_ref, one_ref, other_ref, up_ref, down_ref, up_out, down_out):
    plane = plane_ref[0]

    def merge_into(mine, came, out, valid):
        mine_lse = join_lse(mine[heads * HD :, :])
        came_lse = jnp.where(valid, join_lse(came[heads * HD :, :]), ABSENT)
        peak = jnp.maximum(mine_lse, came_lse)
        mine_weight, came_weight = jnp.exp2(mine_lse - peak), jnp.exp2(came_lse - peak)
        total = mine_weight + came_weight
        mine_weight, came_weight = mine_weight / total, came_weight / total
        for head in range(heads):
            at = slice(head * HD, (head + 1) * HD)
            mixed = mine[at, :].astype(jnp.float32) * mine_weight[head : head + 1]
            mixed += came[at, :].astype(jnp.float32) * came_weight[head : head + 1]
            out[at, :] = mixed.astype(jnp.bfloat16)
        out[heads * HD :, :] = split_lse(peak + jnp.log2(total))

    @pl.when(plane % 2 == 0)
    def _():
        merge_into(one_ref, up_ref, up_out, plane > 0)
        merge_into(other_ref, down_ref, down_out, plane < planes - 1)

    @pl.when(plane % 2 == 1)
    def _():
        merge_into(other_ref, up_ref, up_out, plane > 0)
        merge_into(one_ref, down_ref, down_out, plane < planes - 1)


def merged(plane, planes, heads, *messages):
    spec = pl.BlockSpec(memory_space=pltpu.VMEM)
    size = math.prod(messages[0].shape)
    return pl.pallas_call(
        partial(merge, planes, heads),
        out_shape=[jax.ShapeDtypeStruct(messages[0].shape, jnp.bfloat16)] * 2,
        in_specs=[pl.BlockSpec(memory_space=pltpu.SMEM)] + [spec] * 4,
        out_specs=[spec] * 2,
        cost_estimate=pl.CostEstimate(flops=8 * size, bytes_accessed=12 * size, transcendentals=0),
        compiler_params=pltpu.CompilerParams(vmem_limit_bytes=VMEM),
        name="merge",
    )(plane, *messages)


def finish(planes, heads, chained, plane_ref, own_ref, own_lse_ref, gain_ref, *refs):
    messages, (out_ref, squares_ref) = refs[:-2], refs[-2:]
    plane = plane_ref[0]
    lses = [own_lse_ref[...]] + [join_lse(message[heads * HD :, :]) for message in messages]
    if chained:
        lses[1] = jnp.where(plane > 0, lses[1], ABSENT)
        lses[2] = jnp.where(plane < planes - 1, lses[2], ABSENT)
    peak = lses[0]
    for lse in lses[1:]:
        peak = jnp.maximum(peak, lse)
    weights = [jnp.exp2(lse - peak) for lse in lses]
    total = sum(weights[1:], weights[0])
    weights = [weight / total for weight in weights]
    squares = 0.0
    for head in range(heads):
        at = slice(head * HD, (head + 1) * HD)
        row = slice(head, head + 1)
        mixed = own_ref[at, :] * weights[0][row]
        for message, weight in zip(messages, weights[1:]):
            mixed += message[at, :].astype(jnp.float32) * weight[row]
        squares += jnp.sum(mixed * mixed, axis=0, keepdims=True)
        out_ref[:, at] = mixed.T * gain_ref[:, at]
    squares_ref[...] = squares


def finished(plane, planes, heads, chained, own, own_lse, gain, messages):
    spec = pl.BlockSpec(memory_space=pltpu.VMEM)
    width, rows = own.shape
    return pl.pallas_call(
        partial(finish, planes, heads, chained),
        out_shape=[
            jax.ShapeDtypeStruct((rows, width), jnp.float32),
            jax.ShapeDtypeStruct((1, rows), jnp.float32),
        ],
        in_specs=[pl.BlockSpec(memory_space=pltpu.SMEM)] + [spec] * (3 + len(messages)),
        out_specs=[spec] * 2,
        cost_estimate=pl.CostEstimate(flops=8 * own.size, bytes_accessed=12 * own.size, transcendentals=0),
        compiler_params=pltpu.CompilerParams(vmem_limit_bytes=VMEM),
        name="finish",
    )(plane, own, own_lse, gain, *messages)


def tables(named, global_blocks, plane, corner, planes):
    per_device = named.shape[1]
    count = PLANE * per_device
    owners = plane * PLANE + (corner ^ jnp.arange(PLANE, dtype=jnp.int32))
    blocks = (owners[:, None] * per_device + jnp.arange(per_device, dtype=jnp.int32)[None, :]).reshape(-1)
    times = jnp.sum(named[:, None, :, :] == blocks[None, :, None, None], axis=3)
    times = times + jnp.sum(global_blocks[None, :] == blocks[:, None], axis=1)[None, :, None]
    needed = jnp.max(times, axis=2) > 0
    earlier = jnp.arange(count)[:, None] < jnp.arange(count)[None, :]
    place = jnp.sum(needed[:, :, None] & earlier[None], axis=1)
    chosen = needed[:, None, :] & (place[:, None, :] == jnp.arange(count)[None, :, None])
    spots = jnp.sum(jnp.where(chosen, jnp.arange(count)[None, None, :], 0), axis=2)
    times = jnp.sum(jnp.where(chosen[:, :, :, None], times[:, None, :, :], 0), axis=2)
    bias = jnp.where(times > 0, jnp.log2(times.astype(jnp.float32)), ABSENT)
    bias = jnp.repeat(bias, BLK, axis=2).reshape(planes * PLANE, per_device, per_device * BLK)
    bias = jnp.pad(bias, ((0, 0), (0, up_to(per_device, 8) - per_device), (0, 0)))
    batches = jnp.maximum(-(-jnp.sum(needed, axis=1) // per_device), 1)
    table = jnp.concatenate([plane.reshape(1), batches, spots.reshape(-1)]).astype(jnp.int32)
    return table, bias


def flipped(array, shards, flip):
    return exchange(array, shards, flip * PLANE)


tie = lax.optimization_barrier


def travel(owns, keys, values, own_named, shards, plane):
    planes = shards // PLANE
    arrived, pairs = [], []
    for own, key, value in zip(owns, keys, values):
        arrived.append([flipped(own, shards, planes - order) for order in range(1, planes)])
        pairs.append([exchange(half, shards, flip) if flip else half for flip in range(PLANE) for half in (key, value)])
    return arrived, pairs, [flipped(own_named, shards, planes - order) for order in range(1, planes)]


def travel_on_line(owns, keys, values, own_named, shards, plane):
    groups = range(len(owns))
    ups, downs, near, far, diagonal = ([[] for _ in groups] for _ in range(5))
    rows, width = owns[0].shape
    blocks, names = own_named.shape
    note = jnp.pad(own_named.astype(owns[0].dtype), ((0, up_to(blocks, 16) - blocks), (0, width - names)))
    owns = [jnp.concatenate([owns[0], note], axis=0), *owns[1:]]
    for hop in range(1, 4):
        for c in groups:
            up, down = (ups[c][-1], downs[c][-1]) if hop > 1 else (owns[c], owns[c])
            key, value = keys[c], values[c]
            if hop == 2:
                up, down, *first = tie((up, down, near[c][0], far[c][1]) if TIES[0][c] else (up, down))
                near[c][0], far[c][1] = first or (near[c][0], far[c][1])
            if hop == 3 and c == 0:
                up, down, *diagonal[0] = tie((up, down, *diagonal[0]))
            if hop == 3:
                up, down, *second = tie((up, down, near[c][1], far[c][0]) if TIES[1][c] else (up, down))
                near[c][1], far[c][0] = second or (near[c][1], far[c][0])
            up, down = along(up, shards, 1, hop - 1, 3), along(down, shards, -1, 1, 5 - hop)
            if hop == 1:
                if c and TIES[2]:
                    key, value, *_ = tie((key, value, near[c - 1][1], far[c - 1][0]))
                elif c and TIES[3]:
                    key, value, *_ = tie((key, value, near[c - 1][0], far[c - 1][1]))
                near[c] = [exchange(key, shards, 1), exchange(value, shards, 1)]
                far[c] = [exchange(key, shards, 2), exchange(value, shards, 2)]
            up, down = tie((up, down))
            if hop == 2:
                diagonal[c] = [exchange(near[c][0], shards, 2), exchange(far[c][1], shards, 1)]
            ups[c].append(up)
            downs[c].append(down)
    arrived = [[*ups[c], *downs[c]] for c in groups]
    ups, downs = ([array[rows : rows + blocks, :names] for array in arrays] for arrays in (ups[0], downs[0]))
    named = [jnp.zeros_like(ups[0])] * 3
    for order in range(1, 4):
        for holds, array in chain_sources(order, plane, [None, *ups], [None, *downs]):
            named[order - 1] = jnp.where(holds, array, named[order - 1])
    named = [name.astype(own_named.dtype) for name in named]
    pairs = [[keys[c], values[c], *near[c], *far[c], *diagonal[c]] for c in groups]
    return arrived, pairs, named


def body(queries, key_rows, value_rows, window, random_blocks, global_blocks, norm_gain):
    rows, row_width = queries.shape
    head_count = row_width // HD
    shards = lax.axis_size("seq")
    planes = shards // PLANE
    line = planes == 4
    position = lax.axis_index("seq").astype(jnp.int32)
    plane, corner = position // PLANE, position % PLANE
    own_named = jnp.concatenate([window, random_blocks], axis=1)
    bounds = [0] + [head_count * share // SHARES[-1] * HD for share in SHARES]
    spans = [slice(low, high) for low, high in zip(bounds[:-1], bounds[1:])]
    owns, keys, values = ([array[:, span] for span in spans] for array in (queries, key_rows, value_rows))
    arrived, pairs, named = (travel_on_line if line else travel)(owns, keys, values, own_named, shards, plane)
    table, bias = tables(jnp.stack([own_named, *named]), global_blocks, plane, corner, planes)
    plane = plane.reshape(1)
    gain = norm_gain.reshape(1, row_width)
    parts, own_parts = [], []
    for own, came, pair in zip(owns, arrived, pairs):
        given = table, bias, own, came, pair
        sent = []
        for orders in SPLIT if line else ((*range(1, planes),), (0,)):
            outs = attention("part", orders, *given)
            if 0 in orders:
                *outs, own_part, own_lse = outs
            sent += outs
        parts.append([None, *sent])
        own_parts.append((own_part, own_lse))
    heads = [(span.stop - span.start) // HD for span in spans]
    runs = [None] * len(spans)
    for step in range(1, planes):
        for c in range(len(spans)):
            if line:
                up = down = parts[c][step]
                if step > 1:
                    up, down = merged(plane, planes, heads[c], up, parts[c][planes - step], *runs[c])
                if step == TIEOWN[c]:
                    up, down, *own_parts[c] = tie((up, down, *own_parts[c]))
                runs[c] = tie((along(up, shards, 1, 0, step), along(down, shards, -1, planes - step, planes)))
            elif step == 1:
                runs[c] = [flipped(parts[c][order], shards, planes - order) for order in range(1, planes)]
    attended, squares = [], 0.0
    for c, span in enumerate(spans):
        rows_c, squares_c = finished(plane, planes, heads[c], line, *own_parts[c], gain[:, span], runs[c])
        attended.append(rows_c)
        squares = squares + squares_c
    all_squares = lax.psum(squares.reshape(-1), "head")
    inverse = lax.rsqrt(all_squares / D + 1e-06)
    return (jnp.concatenate(attended, axis=1) * inverse[:, None]).astype(jnp.bfloat16)


def solution(mesh):
    placed = (
        P("seq", "head"),
        P("seq", "head"),
        P("seq", "head"),
        P("seq", None),
        P("seq", None),
        P(),
        P("head"),
    )
    return jax.shard_map(
        body, mesh=mesh, in_specs=placed, out_specs=P("seq", "head"), check_vma=False
    )
```

```python
from functools import partial
import math

import jax
import jax.numpy as jnp
from jax import lax
from jax.experimental import pallas as pl
from jax.experimental.pallas import tpu as pltpu
from jax.sharding import PartitionSpec as P

HD = 128
D = 4096
BLK = 64
PLANE = 4
GROUP = 8
SHARES = (1, 2)
TIES = ((1, 1), (0, 1), 0, 0)
SPLIT = ((1,), (2, 3), (0,))
TIEOWN = (3, 0)
ABSENT = -1e30
NOTHING = 1e-30
VMEM = 40 * 2**20
BIG = 40 * 2**20
SPACE = pltpu.HBM


def up_to(rows, multiple):
    return -(-rows // multiple) * multiple


def exchange(array, shards, flip):
    return lax.ppermute(array, "seq", [(i, i ^ flip) for i in range(shards)])


def along(array, shards, step, first, last):
    pairs = [(z * PLANE + c, (z + step) * PLANE + c) for z in range(first, last) for c in range(PLANE)]
    return lax.ppermute(array, "seq", pairs)


def split_lse(lse):
    high = lse.astype(jnp.bfloat16).astype(jnp.float32)
    rest = lse - high
    middle = rest.astype(jnp.bfloat16).astype(jnp.float32)
    low = rest - middle
    return jnp.concatenate([high, middle, low, jnp.zeros_like(low)], axis=0).astype(jnp.bfloat16)


def join_lse(packed):
    rows = packed.shape[0] // 4
    pieces = packed.astype(jnp.float32)
    return pieces[:rows] + pieces[rows : 2 * rows] + pieces[2 * rows : 3 * rows]


def chain_sources(order, plane, ups, downs):
    low, even = plane < 2, plane % 2 == 0
    if order == 1:
        return ((plane == 0, downs[3]), (plane == 1, downs[1]), (plane == 2, ups[1]), (plane == 3, ups[3]))
    if order == 2:
        return ((low, downs[2]), (jnp.logical_not(low), ups[2]))
    return ((even, downs[1]), (jnp.logical_not(even), ups[1]))


def attend(planes, orders, heads, group, chained, stacked, table_ref, bias_ref, *refs):
    names = iter(refs)
    own = next(names)
    sources = [own] + [next(names) for _ in range(2 * (planes - 1) if chained else planes - 1)]
    ups, downs = sources[:planes], [own] + sources[planes:]
    if stacked:
        pairs = [(ref.at[0], ref.at[1]) for ref in (next(names) for _ in range(PLANE))]
    else:
        pairs = [(next(names), next(names)) for _ in range(PLANE)]
    sent = [order for order in orders if order]
    outs = {order: next(names) for order in sent}
    if 0 in orders:
        own_ref, own_lse_ref = next(names), next(names)
    query_ref, pair_ref, lse_ref, query_sem, pair_sem = names
    plane = table_ref[0]
    rows = own.shape[0]
    blocks = PLANE * rows // BLK
    batch = blocks // PLANE
    lanes = group * HD
    steps = heads // group
    scale = HD**-0.5 * math.log2(math.e)

    def pair_copy(step, j, half):
        at = pl.ds(pl.multiple_of(step * lanes, lanes), lanes)
        return pltpu.make_async_copy(
            pairs[j][half].at[:, at], pair_ref.at[half, pl.ds(j * rows, rows), at], pair_sem.at[step, j, half]
        )

    def query_copy(step, n, source):
        at = pl.ds(pl.multiple_of(step * lanes, lanes), lanes)
        return pltpu.make_async_copy(source.at[pl.ds(0, rows), at], query_ref.at[n, :, at], query_sem.at[step, n])

    for step in range(steps):
        for n, order in enumerate(orders):
            if order == 0 or not chained:
                query_copy(step, n, sources[order]).start()
            else:
                for holds, source in chain_sources(order, plane, ups, downs):
                    pl.when(holds)(query_copy(step, n, source).start)
        for j in range(PLANE):
            for half in range(2):
                pair_copy(step, j, half).start()

    def one_step(step, carry):
        for n in range(len(orders)):
            query_copy(step, n, own).wait()
        for j in range(PLANE):
            for half in range(2):
                pair_copy(step, j, half).wait()
        at = pl.ds(pl.multiple_of(step * lanes, lanes), lanes)
        for n, order in enumerate(orders):
            query = query_ref[n, :, at]
            count = table_ref[1 + order]

            def batch_scores(i):
                start = 1 + planes + order * blocks + i * batch
                spots = [pl.ds(pl.multiple_of(table_ref[start + b] * BLK, BLK), BLK) for b in range(batch)]
                keys = jnp.concatenate([pair_ref[0, spot, at] for spot in spots], axis=0)
                values = jnp.concatenate([pair_ref[1, spot, at] for spot in spots], axis=0)
                bias = bias_ref[order * PLANE + i][:batch]
                scores = []
                for h in range(group):
                    of = slice(h * HD, (h + 1) * HD)
                    product = lax.dot_general(
                        keys[:, of], query[:, of], (((1,), (1,)), ((), ())), preferred_element_type=jnp.float32
                    )
                    scores.append(product.reshape(batch, BLK, rows))
                return scores, bias, values

            def highest(scores, bias):
                top = jnp.max(scores.reshape(batch, BLK // 8, 8, rows), axis=1) * scale + bias[:, None, :]
                return jnp.max(jnp.max(top, axis=0), axis=0, keepdims=True)

            def weigh(scores, bias, peak, values, h):
                weight = jnp.exp2(scores * scale - (peak - bias)[:, None, :])
                total = jnp.sum(weight.reshape(batch * BLK, rows), axis=0, keepdims=True)
                part = lax.dot_general(
                    values[:, h * HD : (h + 1) * HD],
                    weight.astype(jnp.bfloat16).reshape(batch * BLK, rows),
                    (((0,), (0,)), ((), ())),
                    preferred_element_type=jnp.float32,
                )
                return total, part

            def first():
                scores, bias, values = batch_scores(0)
                state = []
                for h in range(group):
                    peak = jnp.maximum(highest(scores[h], bias), ABSENT / 2)
                    state.append((peak, *weigh(scores[h], bias, peak, values, h)))
                return tuple(state)

            def more(i, state):
                scores, bias, values = batch_scores(i)
                after = []
                for h in range(group):
                    peak, total, part = state[h]
                    higher = jnp.maximum(peak, highest(scores[h], bias))
                    shrink = jnp.exp2(peak - higher)
                    added, extra = weigh(scores[h], bias, higher, values, h)
                    after.append((higher, total * shrink + added, part * shrink + extra))
                return tuple(after)

            state = lax.fori_loop(1, count, more, first())
            for h in range(group):
                peak, total, part = state[h]
                total = jnp.maximum(total, NOTHING)
                head = step * group + h
                part = part * (1.0 / total)
                lse_ref[n, pl.ds(head, 1), :] = peak + jnp.log2(total)
                to = pl.ds(pl.multiple_of(head * HD, HD), HD)
                if order == 0:
                    own_ref[to, :] = part
                else:
                    outs[order][to, :] = part.astype(jnp.bfloat16)
        return carry

    lax.fori_loop(0, steps, one_step, 0)
    for n, order in enumerate(orders):
        if order == 0:
            own_lse_ref[...] = lse_ref[n]
        else:
            outs[order][heads * HD :, :] = split_lse(lse_ref[n])


def attention(name, orders, table, bias, own, arrived, pairs):
    rows, width = own.shape
    heads, planes = width // HD, bias.shape[0] // PLANE
    chained, stacked = len(arrived) > planes - 1, len(pairs) == PLANE
    group = math.gcd(heads, GROUP)
    lse_rows = up_to(heads, 8)
    anywhere, whole = pl.BlockSpec(memory_space=SPACE), pl.BlockSpec(memory_space=pltpu.VMEM)
    message = jax.ShapeDtypeStruct((width + 4 * lse_rows, rows), jnp.bfloat16)
    outs = [message for order in orders if order]
    if 0 in orders:
        outs += [jax.ShapeDtypeStruct((width, rows), jnp.float32), jax.ShapeDtypeStruct((lse_rows, rows), jnp.float32)]
    products = heads * len(orders) * PLANE * rows * rows // 2
    return pl.pallas_call(
        partial(attend, planes, orders, heads, group, chained, stacked),
        out_shape=outs,
        in_specs=[pl.BlockSpec(memory_space=pltpu.SMEM), whole] + [anywhere] * (1 + len(arrived) + len(pairs)),
        out_specs=[whole] * len(outs),
        scratch_shapes=[
            pltpu.VMEM((len(orders), rows, width), jnp.bfloat16),
            pltpu.VMEM((2, PLANE * rows, width), jnp.bfloat16),
            pltpu.VMEM((len(orders), lse_rows, rows), jnp.float32),
            pltpu.SemaphoreType.DMA((heads // group, len(orders))),
            pltpu.SemaphoreType.DMA((heads // group, PLANE, 2)),
        ],
        cost_estimate=pl.CostEstimate(
            flops=4 * products * HD, bytes_accessed=8 * 2**20, transcendentals=products
        ),
        compiler_params=pltpu.CompilerParams(vmem_limit_bytes=BIG),
        name=name,
    )(table, bias, own, *arrived, *pairs)


def merge(planes, heads, plane_ref, one_ref, other_ref, up_ref, down_ref, up_out, down_out):
    plane = plane_ref[0]

    def merge_into(mine, came, out, valid):
        mine_lse = join_lse(mine[heads * HD :, :])
        came_lse = jnp.where(valid, join_lse(came[heads * HD :, :]), ABSENT)
        peak = jnp.maximum(mine_lse, came_lse)
        mine_weight, came_weight = jnp.exp2(mine_lse - peak), jnp.exp2(came_lse - peak)
        total = mine_weight + came_weight
        mine_weight, came_weight = mine_weight / total, came_weight / total
        for head in range(heads):
            at = slice(head * HD, (head + 1) * HD)
            mixed = mine[at, :].astype(jnp.float32) * mine_weight[head : head + 1]
            mixed += came[at, :].astype(jnp.float32) * came_weight[head : head + 1]
            out[at, :] = mixed.astype(jnp.bfloat16)
        out[heads * HD :, :] = split_lse(peak + jnp.log2(total))

    @pl.when(plane % 2 == 0)
    def _():
        merge_into(one_ref, up_ref, up_out, plane > 0)
        merge_into(other_ref, down_ref, down_out, plane < planes - 1)

    @pl.when(plane % 2 == 1)
    def _():
        merge_into(other_ref, up_ref, up_out, plane > 0)
        merge_into(one_ref, down_ref, down_out, plane < planes - 1)


def merged(plane, planes, heads, *messages):
    spec = pl.BlockSpec(memory_space=pltpu.VMEM)
    size = math.prod(messages[0].shape)
    return pl.pallas_call(
        partial(merge, planes, heads),
        out_shape=[jax.ShapeDtypeStruct(messages[0].shape, jnp.bfloat16)] * 2,
        in_specs=[pl.BlockSpec(memory_space=pltpu.SMEM)] + [spec] * 4,
        out_specs=[spec] * 2,
        cost_estimate=pl.CostEstimate(flops=8 * size, bytes_accessed=12 * size, transcendentals=0),
        compiler_params=pltpu.CompilerParams(vmem_limit_bytes=VMEM),
        name="merge",
    )(plane, *messages)


def finish(planes, heads, chained, plane_ref, own_ref, own_lse_ref, gain_ref, *refs):
    messages, (out_ref, squares_ref) = refs[:-2], refs[-2:]
    plane = plane_ref[0]
    lses = [own_lse_ref[...]] + [join_lse(message[heads * HD :, :]) for message in messages]
    if chained:
        lses[1] = jnp.where(plane > 0, lses[1], ABSENT)
        lses[2] = jnp.where(plane < planes - 1, lses[2], ABSENT)
    peak = lses[0]
    for lse in lses[1:]:
        peak = jnp.maximum(peak, lse)
    weights = [jnp.exp2(lse - peak) for lse in lses]
    total = sum(weights[1:], weights[0])
    weights = [weight / total for weight in weights]
    squares = 0.0
    for head in range(heads):
        at = slice(head * HD, (head + 1) * HD)
        row = slice(head, head + 1)
        mixed = own_ref[at, :] * weights[0][row]
        for message, weight in zip(messages, weights[1:]):
            mixed += message[at, :].astype(jnp.float32) * weight[row]
        squares += jnp.sum(mixed * mixed, axis=0, keepdims=True)
        out_ref[:, at] = mixed.T * gain_ref[:, at]
    squares_ref[...] = squares


def finished(plane, planes, heads, chained, own, own_lse, gain, messages):
    spec = pl.BlockSpec(memory_space=pltpu.VMEM)
    width, rows = own.shape
    return pl.pallas_call(
        partial(finish, planes, heads, chained),
        out_shape=[
            jax.ShapeDtypeStruct((rows, width), jnp.float32),
            jax.ShapeDtypeStruct((1, rows), jnp.float32),
        ],
        in_specs=[pl.BlockSpec(memory_space=pltpu.SMEM)] + [spec] * (3 + len(messages)),
        out_specs=[spec] * 2,
        cost_estimate=pl.CostEstimate(flops=8 * own.size, bytes_accessed=12 * own.size, transcendentals=0),
        compiler_params=pltpu.CompilerParams(vmem_limit_bytes=VMEM),
        name="finish",
    )(plane, own, own_lse, gain, *messages)


def tables(named, global_blocks, plane, corner, planes):
    per_device = named.shape[1]
    count = PLANE * per_device
    owners = plane * PLANE + (corner ^ jnp.arange(PLANE, dtype=jnp.int32))
    blocks = (owners[:, None] * per_device + jnp.arange(per_device, dtype=jnp.int32)[None, :]).reshape(-1)
    times = jnp.sum(named[:, None, :, :] == blocks[None, :, None, None], axis=3)
    times = times + jnp.sum(global_blocks[None, :] == blocks[:, None], axis=1)[None, :, None]
    needed = jnp.max(times, axis=2) > 0
    earlier = jnp.arange(count)[:, None] < jnp.arange(count)[None, :]
    place = jnp.sum(needed[:, :, None] & earlier[None], axis=1)
    chosen = needed[:, None, :] & (place[:, None, :] == jnp.arange(count)[None, :, None])
    spots = jnp.sum(jnp.where(chosen, jnp.arange(count)[None, None, :], 0), axis=2)
    times = jnp.sum(jnp.where(chosen[:, :, :, None], times[:, None, :, :], 0), axis=2)
    bias = jnp.where(times > 0, jnp.log2(times.astype(jnp.float32)), ABSENT)
    bias = jnp.repeat(bias, BLK, axis=2).reshape(planes * PLANE, per_device, per_device * BLK)
    bias = jnp.pad(bias, ((0, 0), (0, up_to(per_device, 8) - per_device), (0, 0)))
    batches = jnp.maximum(-(-jnp.sum(needed, axis=1) // per_device), 1)
    table = jnp.concatenate([plane.reshape(1), batches, spots.reshape(-1)]).astype(jnp.int32)
    return table, bias


def flipped(array, shards, flip):
    return exchange(array, shards, flip * PLANE)


tie = lax.optimization_barrier


def travel(owns, keys, values, own_named, shards, plane):
    planes = shards // PLANE
    arrived, pairs = [], []
    for own, key, value in zip(owns, keys, values):
        arrived.append([flipped(own, shards, planes - order) for order in range(1, planes)])
        pairs.append([exchange(half, shards, flip) if flip else half for flip in range(PLANE) for half in (key, value)])
    return arrived, pairs, [flipped(own_named, shards, planes - order) for order in range(1, planes)]


def travel_on_line(owns, keys, values, own_named, shards, plane):
    groups = range(len(owns))
    ups, downs, near, far, diagonal = ([[] for _ in groups] for _ in range(5))
    rows, width = owns[0].shape
    blocks, names = own_named.shape
    note = jnp.pad(own_named.astype(owns[0].dtype), ((0, up_to(blocks, 16) - blocks), (0, width - names)))
    owns = [jnp.concatenate([owns[0], note], axis=0), *owns[1:]]
    for hop in range(1, 4):
        for c in groups:
            up, down = (ups[c][-1], downs[c][-1]) if hop > 1 else (owns[c], owns[c])
            key, value = keys[c], values[c]
            if hop == 2:
                up, down, *first = tie((up, down, near[c][0], far[c][1]) if TIES[0][c] else (up, down))
                near[c][0], far[c][1] = first or (near[c][0], far[c][1])
            if hop == 3 and c == 0:
                up, down, *diagonal[0] = tie((up, down, *diagonal[0]))
            if hop == 3:
                up, down, *second = tie((up, down, near[c][1], far[c][0]) if TIES[1][c] else (up, down))
                near[c][1], far[c][0] = second or (near[c][1], far[c][0])
            up, down = along(up, shards, 1, hop - 1, 3), along(down, shards, -1, 1, 5 - hop)
            if hop == 1:
                if c and TIES[2]:
                    key, value, *_ = tie((key, value, near[c - 1][1], far[c - 1][0]))
                elif c and TIES[3]:
                    key, value, *_ = tie((key, value, near[c - 1][0], far[c - 1][1]))
                near_key, far_value = exchange(key, shards, 1), exchange(value, shards, 2)
                far_key, near_value = exchange(key, shards, 2), exchange(value, shards, 1)
                near[c], far[c] = [near_key, near_value], [far_key, far_value]
            up, down = tie((up, down))
            if hop == 2:
                diagonal[c] = [exchange(near[c][0], shards, 2), exchange(far[c][1], shards, 1)]
            ups[c].append(up)
            downs[c].append(down)
    arrived = [[*ups[c], *downs[c]] for c in groups]
    ups, downs = ([array[rows : rows + blocks, :names] for array in arrays] for arrays in (ups[0], downs[0]))
    named = [jnp.zeros_like(ups[0])] * 3
    for order in range(1, 4):
        for holds, array in chain_sources(order, plane, [None, *ups], [None, *downs]):
            named[order - 1] = jnp.where(holds, array, named[order - 1])
    named = [name.astype(own_named.dtype) for name in named]
    pairs = [[keys[c], values[c], *near[c], *far[c], *diagonal[c]] for c in groups]
    return arrived, pairs, named


def body(queries, key_rows, value_rows, window, random_blocks, global_blocks, norm_gain):
    rows, row_width = queries.shape
    head_count = row_width // HD
    shards = lax.axis_size("seq")
    planes = shards // PLANE
    line = planes == 4
    position = lax.axis_index("seq").astype(jnp.int32)
    plane, corner = position // PLANE, position % PLANE
    own_named = jnp.concatenate([window, random_blocks], axis=1)
    bounds = [0] + [head_count * share // SHARES[-1] * HD for share in SHARES]
    spans = [slice(low, high) for low, high in zip(bounds[:-1], bounds[1:])]
    owns, keys, values = ([array[:, span] for span in spans] for array in (queries, key_rows, value_rows))
    arrived, pairs, named = (travel_on_line if line else travel)(owns, keys, values, own_named, shards, plane)
    table, bias = tables(jnp.stack([own_named, *named]), global_blocks, plane, corner, planes)
    plane = plane.reshape(1)
    gain = norm_gain.reshape(1, row_width)
    parts, own_parts = [], []
    for own, came, pair in zip(owns, arrived, pairs):
        given = table, bias, own, came, pair
        sent = []
        for orders in SPLIT if line else ((*range(1, planes),), (0,)):
            outs = attention("part", orders, *given)
            if 0 in orders:
                *outs, own_part, own_lse = outs
            sent += outs
        parts.append([None, *sent])
        own_parts.append((own_part, own_lse))
    heads = [(span.stop - span.start) // HD for span in spans]
    runs = [None] * len(spans)
    for step in range(1, planes):
        for c in range(len(spans)):
            if line:
                up = down = parts[c][step]
                if step > 1:
                    up, down = merged(plane, planes, heads[c], up, parts[c][planes - step], *runs[c])
                if step == TIEOWN[c]:
                    up, down, *own_parts[c] = tie((up, down, *own_parts[c]))
                runs[c] = tie((along(up, shards, 1, 0, step), along(down, shards, -1, planes - step, planes)))
            elif step == 1:
                runs[c] = [flipped(parts[c][order], shards, planes - order) for order in range(1, planes)]
    attended, squares = [], 0.0
    for c, span in enumerate(spans):
        rows_c, squares_c = finished(plane, planes, heads[c], line, *own_parts[c], gain[:, span], runs[c])
        attended.append(rows_c)
        squares = squares + squares_c
    all_squares = lax.psum(squares.reshape(-1), "head")
    inverse = lax.rsqrt(all_squares / D + 1e-06)
    return (jnp.concatenate(attended, axis=1) * inverse[:, None]).astype(jnp.bfloat16)


def solution(mesh):
    placed = (
        P("seq", "head"),
        P("seq", "head"),
        P("seq", "head"),
        P("seq", None),
        P("seq", None),
        P(),
        P("head"),
    )
    return jax.shard_map(
        body, mesh=mesh, in_specs=placed, out_specs=P("seq", "head"), check_vma=False
    )
```
